512 devices in a mesh: gx: 32 (over z, core), gy: 16 (over y, x).
Axes of the slice: x: 4, y: 4, z: 16, core: 2. Of those that a mesh axis runs over, the one named last changes fastest.
Arguments:
- load_cases: bfloat16 [32, 16, 1024, 128], P('gx', 'gy')
- schur_blocks: bfloat16 [32, 16, 1024, 1024], P('gx', 'gy'), as said below
- local_inverse: bfloat16 [32, 16, 1024, 1024], P('gx', 'gy'), as said below
- coarse_basis: bfloat16 [32, 16, 8, 1024], P('gx', 'gy'), may hold values from -0.375 to 0.375
- corner_ids: int32 [32, 16, 8], P('gx', 'gy'), may hold values from 0 to 1023, as said below
- coarse_inverse: bfloat16 [1024, 1024], P('gy'), as said below
Outputs:
- solution_field: bfloat16 [32, 16, 1024, 128], P('gx', 'gy')
- residual: bfloat16 [32, 16, 1024, 128], P('gx', 'gy')
The draws below stay inside these ranges and needn't reach their ends.
Inputs may be any that keep to these rules, and one draw needn't show every extreme that they name: `corner_ids`: coarse unknowns sit at grid vertices, 2 to a vertex, vertices and components numbered by one fixed permutation. Slot k of subdomain (a, b) names component k mod 2 of vertex ((a + c // 2) mod 32, (b + c mod 2) mod 16) with c = k // 2; so every coarse unknown is named by exactly 4 subdomains. `schur_blocks`: every subdomain block is symmetric. `local_inverse`: symmetric per subdomain. `coarse_inverse`: Symmetric.
All inputs are finite; a program needn't handle non-finite values.
Results may differ from the reference program's by a relative error of at most 0.01.
The reference program's roundings to bfloat16 on the way (of `schur_part`, `scaled`, `coarse_total`, `coarse_solution` and `blended`) count: a program that leaves them out, or rounds other values in their place, can miss the bound.
Values may be sent and summed in bfloat16 or wider, within the bound.
No kernel may reach another device: no remote copies, remote signals or barrier semaphores. Data moves between devices by JAX's collectives and lax.ppermute only.
A program may use at most 64 MiB of HBM per device.

```python
import jax
import jax.numpy as jnp
from jax import lax

NI = 1024
NRHS = 128
CPV = 2
ITERS = 3
NC = 8
NCG = 1024
N_GX = 32
N_GY = 16


def off_diagonal(key, shape, amount):
    order = shape[-1]
    noise = jax.random.uniform(key, shape, jnp.float32, -1.0, 1.0)
    return (noise + jnp.swapaxes(noise, -1, -2)) * (0.5 * amount / jnp.sqrt(order * 1.0))


def with_diagonal(matrix, diagonal):
    order = matrix.shape[-1]
    identity = (jnp.arange(order)[:, None] == jnp.arange(order)[None, :]).astype(jnp.float32)
    return matrix + identity * diagonal[..., None]


def draw_load_cases(key, part):
    key = jax.random.fold_in(key, 1)
    shape = (N_GX, N_GY, NI, NRHS)
    rising = 1.0 + 2.0 * jnp.arange(N_GX, dtype=jnp.float32) / (N_GX - 1)
    scale = rising[:, None, None, None]
    base = jax.random.normal(key, shape, jnp.float32)
    return (base * scale).astype(jnp.bfloat16)


def draw_schur_blocks(key, part):
    key = jax.random.fold_in(key, 2)
    first, second = jax.random.split(key)
    shape = (N_GX, N_GY, NI, NI)
    diagonal = jnp.exp(jax.random.uniform(second, shape[:-1], jnp.float32, 0.0, 1.386))
    return with_diagonal(off_diagonal(first, shape, 0.6), diagonal).astype(jnp.bfloat16)


def draw_local_inverse(key, part):
    key = jax.random.fold_in(key, 3)
    first, second = jax.random.split(key)
    shape = (N_GX, N_GY, NI, NI)
    diagonal = jnp.exp(jax.random.uniform(second, shape[:-1], jnp.float32, -1.2, 0.18))
    return with_diagonal(off_diagonal(first, shape, 0.15), diagonal).astype(jnp.bfloat16)


def draw_coarse_inverse(key, part):
    key = jax.random.fold_in(key, 4)
    first, second = jax.random.split(key)
    shape = (NCG, NCG)
    diagonal = jnp.exp(jax.random.uniform(second, shape[:-1], jnp.float32, 0.4, 1.8))
    return with_diagonal(off_diagonal(first, shape, 1.8), diagonal).astype(jnp.bfloat16)


def draw_corner_ids(key, part):
    key = jax.random.fold_in(key, 5)
    numbering = jax.random.permutation(key, NCG).astype(jnp.int32)
    first = jnp.arange(N_GX, dtype=jnp.int32)[:, None, None]
    second = jnp.arange(N_GY, dtype=jnp.int32)[None, :, None]
    slot = jnp.arange(NC, dtype=jnp.int32)[None, None, :]
    corner = slot // CPV
    component = slot % CPV
    vertex_x = (first + corner // 2) % N_GX
    vertex_y = (second + corner % 2) % N_GY
    geometric = (vertex_x * N_GY + vertex_y) * CPV + component
    return numbering[geometric].astype(jnp.int32)


def block_levels(key, extent, cuts, smallest, largest):
    loudness = 1.0
    for position, blocks in cuts:
        draws = jax.random.uniform(jax.random.fold_in(jax.random.fold_in(key, 6), position), (blocks,), jnp.float32, smallest / len(cuts), largest / len(cuts))
        loudness = loudness * jnp.repeat(jnp.exp(draws), extent[position] // blocks).reshape((-1,) + (1,) * (len(extent) - 1 - position))
    return loudness


def gaussian(own_key, shape, deviation, reach, shards=(), held_as=jnp.bfloat16):
    factor_of = block_levels(own_key, shape, shards, -0.22, 0.18) if shards else 1.0
    values = jax.random.normal(own_key, shape, jnp.float32) * deviation * factor_of
    return jnp.minimum(jnp.maximum(values, -reach), reach).astype(held_as)


def setup_inputs(seed: int = 0) -> dict:
    keys = jax.random.split(jax.random.key(seed), 7)
    load_cases = draw_load_cases(jax.random.fold_in(keys[6], 71), 0)
    schur_blocks = draw_schur_blocks(jax.random.fold_in(keys[6], 71), 0)
    local_inverse = draw_local_inverse(jax.random.fold_in(keys[6], 71), 0)
    coarse_basis = gaussian(keys[3], (N_GX, N_GY, NC, NI), (NI // 4) ** -0.5, 0.375, ((0, 32), (1, 16)))
    corner_ids = draw_corner_ids(jax.random.fold_in(keys[6], 71), 0)
    coarse_inverse = draw_coarse_inverse(jax.random.fold_in(keys[6], 71), 0)
    return dict(load_cases=load_cases, schur_blocks=schur_blocks, local_inverse=local_inverse, coarse_basis=coarse_basis, corner_ids=corner_ids, coarse_inverse=coarse_inverse)


def face_weights():
    rows = NI // 4
    first = jnp.arange(N_GX)[:, None] + jnp.zeros((1, N_GY), jnp.int32)
    second = jnp.zeros((N_GX, 1), jnp.int32) + jnp.arange(N_GY)[None, :]
    values = [jnp.where(first > 0, 0.5, 1.0), jnp.where(first < N_GX - 1, 0.5, 1.0),
              jnp.where(second > 0, 0.5, 1.0), jnp.where(second < N_GY - 1, 0.5, 1.0)]
    blocks = [jnp.broadcast_to(value[:, :, None, None].astype(jnp.float32), (N_GX, N_GY, rows, 1)) for value in values]
    return jnp.concatenate(blocks, axis=2)


def assemble(local):
    rows = NI // 4
    low_x = local[:, :, :rows]
    high_x = local[:, :, rows:2 * rows]
    low_y = local[:, :, 2 * rows:3 * rows]
    high_y = local[:, :, 3 * rows:]
    zero_x = jnp.zeros_like(low_x[:1])
    zero_y = jnp.zeros_like(low_y[:, :1])
    below_x = jnp.concatenate([zero_x, high_x[:-1]], axis=0)
    above_x = jnp.concatenate([low_x[1:], zero_x], axis=0)
    below_y = jnp.concatenate([zero_y, high_y[:, :-1]], axis=1)
    above_y = jnp.concatenate([low_y[:, 1:], zero_y], axis=1)
    return local + jnp.concatenate([below_x, above_x, below_y, above_y], axis=2)


def multiply(operands):
    return jnp.dot(operands[0], operands[1], preferred_element_type=jnp.float32)


def local_products(blocks, vectors):
    flat_blocks = blocks.reshape(N_GX * N_GY, NI, NI)
    flat_vectors = vectors.reshape(N_GX * N_GY, NI, NRHS)
    result = lax.map(multiply, (flat_blocks, flat_vectors))
    return result.reshape(N_GX, N_GY, NI, NRHS)


def reference(load_cases, schur_blocks, local_inverse, coarse_basis, corner_ids, coarse_inverse):
    weight = face_weights()
    basis_wide = coarse_basis.astype(jnp.float32)

    def inner(first, second):
        return jnp.sum(weight * first * second, axis=(0, 1, 2))

    def image(direction):
        schur_part = local_products(schur_blocks, direction.astype(jnp.bfloat16)).astype(jnp.bfloat16)
        schur_part = lax.optimization_barrier(schur_part)
        return assemble(schur_part.astype(jnp.float32))

    def precondition(remainder):
        scaled = (weight * remainder).astype(jnp.bfloat16)
        local_part = local_products(local_inverse, scaled)
        coarse_terms = jnp.einsum("abci,abir->abcr", basis_wide, scaled.astype(jnp.float32),
                                  precision=lax.Precision.HIGHEST)
        coarse_total = jnp.zeros((NCG, NRHS), jnp.float32).at[corner_ids.reshape(-1)].add(
            coarse_terms.reshape(-1, NRHS))
        coarse_solution = jnp.dot(coarse_inverse, coarse_total.astype(jnp.bfloat16),
                                  preferred_element_type=jnp.float32).astype(jnp.bfloat16)
        picked = coarse_solution[corner_ids].astype(jnp.float32)
        coarse_part = jnp.einsum("abci,abcr->abir", basis_wide, picked, precision=lax.Precision.HIGHEST)
        blended = (weight * (local_part + coarse_part)).astype(jnp.bfloat16)
        blended = lax.optimization_barrier(blended)
        return assemble(blended.astype(jnp.float32))

    residual = load_cases.astype(jnp.float32)
    solution_field = jnp.zeros_like(residual)
    search = precondition(residual)
    direction = search
    rz_now = inner(residual, search)
    for iteration in range(ITERS):
        product = image(direction)
        alpha = rz_now / inner(direction, product)
        solution_field = solution_field + alpha * direction
        residual = residual - alpha * product
        if iteration + 1 < ITERS:
            search = precondition(residual)
            rz_next = inner(residual, search)
            direction = search + (rz_next / rz_now) * direction
            rz_now = rz_next
    return solution_field.astype(jnp.bfloat16), residual.astype(jnp.bfloat16)
```

```python
import jax
import jax.numpy as jnp
from jax import lax
from jax.experimental import pallas as pl
from jax.experimental.pallas import tpu as pltpu
from jax.sharding import PartitionSpec as P

F32 = jnp.float32
BF16 = jnp.bfloat16
NI = 1024
FACE = 256
R = 128
NX = 32
NY = 16
SL = R // NY
NCG = 1024
WIN = 32

VMEM = pl.BlockSpec(memory_space=pltpu.VMEM)
SMEM = pl.BlockSpec(memory_space=pltpu.SMEM)


def call(kernel, args, outs, scratch=(), smem=0, flops=0):
    size = sum(a.size * a.dtype.itemsize for a in args)
    return pl.pallas_call(
        kernel,
        out_shape=tuple(jax.ShapeDtypeStruct(s, d) for s, d in outs),
        in_specs=[SMEM] * smem + [VMEM] * (len(args) - smem),
        out_specs=tuple(VMEM for _ in outs),
        scratch_shapes=list(scratch),
        compiler_params=pltpu.CompilerParams(vmem_limit_bytes=32 * 1024 * 1024),
        cost_estimate=pl.CostEstimate(flops=flops, bytes_accessed=size, transcendentals=0),
    )(*args)


def rows(i):
    return slice(FACE * i, FACE * (i + 1))


def dot(a, b):
    return jnp.dot(a, b, preferred_element_type=F32)


def lanes(shape):
    return lax.broadcasted_iota(jnp.int32, shape, len(shape) - 1)


def rolled(value, shift):
    shift = shift % 128
    return value if shift == 0 else pltpu.roll(value, shift, value.ndim - 1)


def total(value):
    return jnp.sum(value, axis=0, keepdims=True)


def start_kernel(wt, ids, load, inverse, basis, own, l_out, f0, f1, f2, f3, msg_out, table):
    scaled = [(load[rows(i)].astype(F32) * wt[i]).astype(BF16) for i in range(4)]
    scaled = jnp.concatenate(scaled, axis=0)
    for i, face in enumerate((f0, f1, f2, f3)):
        local = wt[i] * dot(inverse[rows(i)], scaled)
        l_out[rows(i)] = local
        face[0:FACE] = local
        face[FACE : FACE + 8] = basis[:, FACE * i : FACE * i + 128].astype(F32)
        face[FACE + 8 : FACE + 16] = basis[:, FACE * i + 128 : FACE * (i + 1)].astype(F32)
    table[...] = jnp.zeros((128, 128), F32)
    table[0:WIN] = dot(own[...], scaled)
    for c in range(2):
        table[64 + c : 65 + c] = jnp.full((1, 128), ids[c].astype(F32))
    msg_out[...] = jnp.transpose(table[...]).reshape(NY, SL, 128)


def place(out, base, column, piece, dx0, dy0):
    width = piece.shape[1]
    for cx in range(2):
        for cy in range(2):
            row = base + (dy0 + cy) * 8 + (dx0 + cx) * 2
            slot = 4 * cx + 2 * cy
            out[row : row + 2, column : column + width] = piece[slot : slot + 2]


def window_kernel(basis, f0, f1, f2, f3, b_out, bt_out, table):
    table[...] = jnp.zeros((2 * WIN, NI), F32)
    place(table, 0, 0, basis[...].astype(F32), 1, 1)
    for i, (face, dx0, dy0) in enumerate(((f0, 0, 1), (f1, 2, 1), (f2, 1, 0), (f3, 1, 2))):
        for h in range(2):
            piece = face[FACE + 8 * h : FACE + 8 * h + 8]
            place(table, WIN, FACE * i + 128 * h, piece, dx0, dy0)
    b_out[...] = table[...].astype(BF16)
    bt_out[...] = jnp.transpose(table[...]).astype(BF16)


def local_kernel(wt, s, f0, f1, f2, f3, inverse, q_out, l_out, g0, g1, g2, g3):
    parts = []
    for i, face in enumerate((f0, f1, f2, f3)):
        q = s[rows(i)].astype(F32) + face[...].astype(F32)
        q_out[rows(i)] = q
        parts.append((wt[i] * q).astype(BF16))
    scaled = jnp.concatenate(parts, axis=0)
    for i, face in enumerate((g0, g1, g2, g3)):
        local = wt[i] * dot(inverse[rows(i)], scaled)
        l_out[rows(i)] = local
        face[...] = local


def arrived(m):
    return jnp.transpose(m[...].reshape(R, 128))


def blended(wt, i, window_t, y, mine, facing):
    y = y[0:WIN].astype(BF16)
    mine = mine + wt[i] * dot(window_t[rows(i), 0:WIN], y)
    facing = facing + wt[i] * dot(window_t[rows(i), WIN:], y)
    return mine.astype(BF16).astype(F32) + facing.astype(BF16).astype(F32)


def split(value):
    high = value.astype(BF16)
    return jnp.concatenate([high, (value - high.astype(F32)).astype(BF16)], axis=1)


def joined(value):
    return value[:, 0:R] + value[:, R:]


def apply_schur(schur, zb, s_out, faces):
    for i, face in enumerate(faces):
        s = joined(dot(schur[rows(i)], zb[...]))
        s_out[rows(i)] = s
        face[...] = s


def window_terms(wt, window, s):
    terms = jnp.zeros((2 * WIN, 2 * R), F32)
    for i in range(4):
        terms += dot(window[:, rows(i)], split(s[rows(i)].astype(F32) * wt[i]))
    return joined(terms[0:WIN] + terms[WIN:])


def send_table(table, msg_out, terms, inner):
    table[...] = jnp.zeros((128, 128), F32)
    table[0:WIN] = terms
    for j, value in enumerate(inner):
        table[WIN + j : WIN + j + 1] = value
    msg_out[...] = jnp.transpose(table[...]).reshape(NY, SL, 128)


def first_kernel(
    wt, m, l0, f0, f1, f2, f3, window_t, window, schur, load,
    z_out, s_out, g0, g1, g2, g3, msg_out, table, zb,
):
    y = arrived(m)
    for i, face in enumerate((f0, f1, f2, f3)):
        z = blended(wt, i, window_t, y, l0[rows(i)], face[0:FACE])
        z_out[rows(i)] = z
        zb[rows(i)] = z.astype(BF16)
    for i, face in enumerate((g0, g1, g2, g3)):
        s = dot(schur[rows(i)], zb[...]).astype(BF16)
        s_out[rows(i)] = s
        face[...] = s
    rz = jnp.zeros((1, R), F32)
    pq = jnp.zeros((1, R), F32)
    for i in range(4):
        z = z_out[rows(i)]
        rz += total(wt[i] * load[rows(i)].astype(F32) * z)
        pq += total(z * s_out[rows(i)].astype(F32))
    send_table(table, msg_out, window_terms(wt, window, s_out), (rz, pq))


def second_kernel(
    wt, m, l0, e0, e1, e2, e3, l1, f0, f1, f2, f3, q0, s0, window_t, window, schur, load,
    z_out, l_out, h0, h1, h2, h3, r_out, s_out, g0, g1, g2, g3, msg_out, got_out, table, zb,
):
    got = arrived(m)
    got_out[...] = got[WIN : WIN + 8]
    alpha = got[WIN : WIN + 1]
    faces = ((e0, f0, h0), (e1, f1, h1), (e2, f2, h2), (e3, f3, h3))
    for i, (before, face, after) in enumerate(faces):
        mine = l0[rows(i)] - alpha * l1[rows(i)]
        facing = before[0:FACE] - alpha * face[...]
        z = blended(wt, i, window_t, got, mine, facing)
        l_out[rows(i)] = mine
        after[...] = facing
        z_out[rows(i)] = z
        zb[rows(i)] = split(z)
        r_out[rows(i)] = load[rows(i)].astype(F32) - alpha * q0[rows(i)]
    apply_schur(schur, zb, s_out, (g0, g1, g2, g3))
    rz = jnp.zeros((1, R), F32)
    zz = jnp.zeros((1, R), F32)
    zq = jnp.zeros((1, R), F32)
    for i in range(4):
        z = z_out[rows(i)]
        rz += total(wt[i] * r_out[rows(i)] * z)
        zz += total(z * s_out[rows(i)])
        zq += total(z * s0[rows(i)].astype(F32))
    send_table(table, msg_out, window_terms(wt, window, s_out), (rz, zz, zq))


def third_kernel(
    wt, m, got0, lm, d0, d1, d2, d3, l1, e0, e1, e2, e3, l2, f0, f1, f2, f3,
    q0, q1, s0, s1, z0, z1, r1, window_t, schur,
    z_out, x_out, p_out, q_out, r_out, s_out, g0, g1, g2, g3, msg_out, got_out, zb,
):
    got = arrived(m)
    got_out[...] = got[WIN : WIN + 8]
    alpha0 = got0[0:1]
    alpha = got[WIN : WIN + 1]
    beta = got[WIN + 1 : WIN + 2]
    faces = ((d0, e0, f0), (d1, e1, f1), (d2, e2, f2), (d3, e3, f3))
    for i, (before, first, second) in enumerate(faces):
        mine = lm[rows(i)] - alpha * (l2[rows(i)] + beta * l1[rows(i)])
        facing = before[...] - alpha * (second[...] + beta * first[...])
        z = blended(wt, i, window_t, got, mine, facing)
        z_out[rows(i)] = z
        zb[rows(i)] = split(z)
        p = z1[rows(i)] + beta * z0[rows(i)]
        q = q1[rows(i)] + beta * q0[rows(i)]
        p_out[rows(i)] = p
        q_out[rows(i)] = q
        x_out[rows(i)] = alpha0 * z0[rows(i)] + alpha * p
        r_out[rows(i)] = r1[rows(i)] - alpha * q
    apply_schur(schur, zb, s_out, (g0, g1, g2, g3))
    rz = jnp.zeros((1, R), F32)
    zz = jnp.zeros((1, R), F32)
    zq = jnp.zeros((1, R), F32)
    for i in range(4):
        z = z_out[rows(i)]
        s = s1[rows(i)] + beta * s0[rows(i)].astype(F32)
        rz += total(wt[i] * r_out[rows(i)] * z)
        zz += total(z * s_out[rows(i)])
        zq += total(z * s)
    inner = jnp.concatenate([rz, zz, zq, jnp.zeros((5, R), F32)], axis=0)
    msg_out[...] = jnp.broadcast_to(inner[None], (NY, 8, R))


def last_kernel(m, got, s, f0, f1, f2, f3, z, p, q, x, r, x_out, r_out):
    inner = jnp.sum(m[...], axis=0)
    rz1 = got[2:3]
    pq1 = got[3:4]
    rz = inner[0:1]
    beta = rz / rz1
    pq = inner[1:2] + 2.0 * beta * inner[2:3] + beta * beta * pq1
    alpha = rz / pq
    for i, face in enumerate((f0, f1, f2, f3)):
        product = s[rows(i)] + face[...] + beta * q[rows(i)]
        direction = z[rows(i)] + beta * p[rows(i)]
        x_out[rows(i)] = (x[rows(i)] + alpha * direction).astype(BF16)
        r_out[rows(i)] = (r[rows(i)] - alpha * product).astype(BF16)


def column_kernel(m, out):
    where = lanes((SL, 128))
    column = jnp.zeros((SL, 128), F32)
    other = jnp.zeros((SL, 128), F32)
    for b in range(NY):
        value = m[b]
        column += rolled(jnp.where(where < WIN, value, 0.0), 8 * (b - 1))
        other += jnp.where((where >= WIN) & (where < 64), value, 0.0)
    both = jnp.concatenate([column, other], axis=0)
    out[...] = jnp.broadcast_to(both[None], (NX, 2 * SL, 128))


def first_column_kernel(m, out):
    where = lanes((SL, 128))
    column = jnp.zeros((SL, 128), F32)
    other = jnp.zeros((SL, 128), F32)
    for b in range(NY):
        value = m[b]
        column += rolled(jnp.where(where < WIN, value, 0.0), 8 * (b - 1))
        named = jnp.where((where >= 64) & (where < 66), value, 0.0)
        other += rolled(named, 8 * b - 64)
    both = jnp.concatenate([column, other], axis=0)
    out[...] = jnp.broadcast_to(both[None], (NX, 2 * SL, 128))


def vertex_sums(m, group):
    place_of = lanes((SL, 128)) % 8 // 2
    result = jnp.zeros((SL, 128), F32)
    for k in range(4):
        value = jnp.zeros((SL, 128), F32)
        for j in range(4):
            value += rolled(m[(4 * group + k - j + 1) % NX, 0:SL], 2 * (k - j))
        result += jnp.where(place_of == k, value, 0.0)
    return result


def reply(out, y, scalars):
    where = lanes((SL, 128))
    rest = jnp.zeros((SL, 128), F32)
    for j, value in enumerate(scalars):
        rest += jnp.where(where == WIN + j, value, 0.0)
    for b in range(NY):
        out[b] = jnp.where(where < WIN, rolled(y, -8 * (b - 1)), rest)


def solve(sums, table, out, scalars):
    y = dot(sums[...].astype(BF16), table[...])
    reply(out, y.astype(BF16).astype(F32), scalars)


def first_solve_kernel(ax, m, inverse, sums, table, out, picked, spread):
    for group in range(8):
        sums[:, 128 * group : 128 * (group + 1)] = vertex_sums(m, group)
    own = jnp.zeros((SL, 128), F32)
    for j in range(4):
        own += rolled(m[(ax[0] + j - 1 + NX) % NX, SL : 2 * SL], 2 * j)
    for i in range(4):
        number = lax.broadcasted_iota(jnp.int32, (FACE, 128), 0).astype(F32) + float(FACE * i)
        spread[rows(i), 0:128] = jnp.where(number == own[0:1], 1.0, 0.0).astype(BF16)
    for i in range(4):
        picked[rows(i)] = dot(inverse[rows(i)], spread[:, 0:128]).astype(BF16)
    lane = lanes((128, 128)).astype(F32)
    for group in range(8):
        named = jnp.zeros((SL, 128), F32)
        for k in range(4):
            named += rolled(m[4 * group + k, SL : 2 * SL], 2 * k)
        named = jnp.transpose(jnp.broadcast_to(named[0:1], (128, 128)))
        for part in range(8):
            spread[128 * group : 128 * (group + 1), 128 * part : 128 * (part + 1)] = jnp.where(
                named == lane + float(128 * part), 1.0, 0.0
            ).astype(BF16)
    for i in range(4):
        table[rows(i)] = dot(spread[rows(i)], picked[...]).astype(BF16)
    solve(sums, table, out, ())


def scalar(value, j):
    where = lanes((SL, 128))
    return jnp.sum(jnp.where(where == WIN + j, value, 0.0), axis=1, keepdims=True)


def second_solve_kernel(m, sums0, table, change, sums, kept, out):
    inner = jnp.sum(m[:, SL : 2 * SL], axis=0)
    rz, pq = (scalar(inner, 0), scalar(inner, 1))
    alpha = rz / pq
    for group in range(8):
        part = slice(128 * group, 128 * (group + 1))
        value = vertex_sums(m, group)
        change[:, part] = value
        sums[:, part] = sums0[:, part] - alpha * value
    kept[...] = jnp.where(lanes((SL, 128)) == 0, rz, pq)
    solve(sums, table, out, (alpha,))


def third_solve_kernel(m, sums1, table, change0, kept, out, sums):
    inner = jnp.sum(m[:, SL : 2 * SL], axis=0)
    rz, zz, zq = (scalar(inner, 0), scalar(inner, 1), scalar(inner, 2))
    beta = rz / kept[:, 0:1]
    pq = zz + 2.0 * beta * zq + beta * beta * kept[:, 1:2]
    alpha = rz / pq
    for group in range(8):
        part = slice(128 * group, 128 * (group + 1))
        value = vertex_sums(m, group) + beta * change0[:, part]
        sums[:, part] = sums1[:, part] - alpha * value
    solve(sums, table, out, (alpha, beta, rz, pq))


def last_column_kernel(m, out):
    out[...] = jnp.broadcast_to(jnp.sum(m[...], axis=0)[None], (NX, 8, R))


def across(faces):
    low_x, high_x, low_y, high_y = faces
    result = []
    for axis, size, low, high in (("gx", NX, low_x, high_x), ("gy", NY, low_y, high_y)):
        up = [(i, i + 1) for i in range(size - 1)]
        down = [(j, i) for i, j in up]
        result.append(lax.ppermute(high, axis, up))
        result.append(lax.ppermute(low, axis, down))
    return result


def swap(value, axis):
    return lax.all_to_all(value, axis, 0, 0, tiled=True)


def body(load_cases, schur_blocks, local_inverse, coarse_basis, corner_ids, coarse_inverse):
    load = load_cases[0, 0]
    schur = schur_blocks[0, 0]
    inverse = local_inverse[0, 0]
    basis = coarse_basis[0, 0]
    ids = corner_ids[0, 0]
    ax = lax.axis_index("gx")
    ay = lax.axis_index("gy")
    shared = jnp.stack([ax > 0, ax < NX - 1, ay > 0, ay < NY - 1])
    wt = jnp.where(shared, 0.5, 1.0).astype(F32)
    gap = jnp.zeros((10, NI), BF16)
    own = jnp.concatenate(
        [gap, basis[0:2], basis[4:6], gap[0:4], basis[2:4], basis[6:8], gap], axis=0
    )
    copies = jnp.broadcast_to(coarse_inverse[None], (NY, NCG // NY, NCG))
    whole = swap(copies, "gy").reshape(NCG, NCG)

    tall = (NI, R)
    msg = ((NY, SL, 128), F32)
    wide = ((NX, 2 * SL, 128), F32)
    block = 2 * NI * NI * R
    table = pltpu.VMEM((128, 128), F32)
    zb = pltpu.VMEM((NI, 2 * R), BF16)
    face = ((FACE, R), F32)
    l0, f0, f1, f2, f3, m = call(
        start_kernel,
        (wt, ids, load, inverse, basis, own),
        [(tall, F32)] + [((FACE + 16, R), F32)] * 4 + [msg],
        [table],
        smem=2,
        flops=block,
    )
    m = swap(m, "gy")
    faces = across((f0, f1, f2, f3))
    (m,) = call(first_column_kernel, (m,), [wide])
    m = swap(m, "gx")
    window, window_t = call(
        window_kernel,
        (basis, *faces),
        [((2 * WIN, NI), BF16), ((NI, 2 * WIN), BF16)],
        [pltpu.VMEM((2 * WIN, NI), F32)],
    )
    sums0, picked, m = call(
        first_solve_kernel,
        (ax.astype(jnp.int32).reshape(1), m, whole),
        [((SL, NCG), F32), ((NCG, 128), BF16), msg],
        [pltpu.VMEM((NCG, 128), BF16), pltpu.VMEM((NCG, NCG), BF16)],
        smem=1,
        flops=2 * block,
    )
    m = swap(m, "gy")
    z0, s0, g0, g1, g2, g3, m = call(
        first_kernel,
        (wt, m, l0, *faces, window_t, window, schur, load),
        [(tall, F32), (tall, BF16)] + [((FACE, R), BF16)] * 4 + [msg],
        [table, pltpu.VMEM(tall, BF16)],
        smem=1,
        flops=block,
    )

    def local(s, sent):
        q, l, h0, h1, h2, h3 = call(
            local_kernel,
            (wt, s, *across(sent), inverse),
            [(tall, F32), (tall, F32)] + [face] * 4,
            smem=1,
            flops=block,
        )
        return q, l, across((h0, h1, h2, h3))

    m = swap(m, "gy")
    q0, l1, faces1 = local(s0, (g0, g1, g2, g3))
    (m,) = call(column_kernel, (m,), [wide])
    m = swap(m, "gx")
    change0, sums1, kept, m = call(
        second_solve_kernel,
        (m, sums0, picked),
        [((SL, NCG), F32), ((SL, NCG), F32), ((SL, 128), F32), msg],
    )
    m = swap(m, "gy")
    z1, lm, d0, d1, d2, d3, r1, s1, g0, g1, g2, g3, m, got0 = call(
        second_kernel,
        (wt, m, l0, *faces, l1, *faces1, q0, s0, window_t, window, schur, load),
        [(tall, F32)] * 2 + [face] * 4 + [(tall, F32)] * 2 + [face] * 4 + [msg, ((8, R), F32)],
        [table, zb],
        smem=1,
        flops=block,
    )

    m = swap(m, "gy")
    q1, l2, faces2 = local(s1, (g0, g1, g2, g3))
    (m,) = call(column_kernel, (m,), [wide])
    m = swap(m, "gx")
    (m,) = call(
        third_solve_kernel,
        (m, sums1, picked, change0, kept),
        [msg],
        [pltpu.VMEM((SL, NCG), F32)],
    )
    m = swap(m, "gy")
    z2, x2, p1, q1, r2, s2, g0, g1, g2, g3, m, got1 = call(
        third_kernel,
        (
            wt, m, got0, lm, d0, d1, d2, d3, l1, *faces1, l2, *faces2,
            q0, q1, s0, s1, z0, z1, r1, window_t, schur,
        ),
        [(tall, F32)] * 6 + [face] * 4 + [((NY, 8, R), F32), ((8, R), F32)],
        [zb],
        smem=1,
        flops=block,
    )

    m = swap(m, "gy")
    faces = across((g0, g1, g2, g3))
    (m,) = call(last_column_kernel, (m,), [((NX, 8, R), F32)])
    m = swap(m, "gx")
    x, r = call(
        last_kernel,
        (m, got1, s2, *faces, z2, p1, q1, x2, r2),
        [(tall, BF16), (tall, BF16)],
    )
    return x[None, None], r[None, None]


def solution(mesh):
    return jax.shard_map(
        body,
        mesh=mesh,
        in_specs=(
            P("gx", "gy", None, None),
            P("gx", "gy", None, None),
            P("gx", "gy", None, None),
            P("gx", "gy", None, None),
            P("gx", "gy", None),
            P("gy", None),
        ),
        out_specs=(P("gx", "gy", None, None), P("gx", "gy", None, None)),
        check_vma=False,
    )
```

```python
from typing import NamedTuple

import jax
import jax.numpy as jnp
from jax import lax
from jax.experimental import pallas as pl
from jax.experimental.pallas import tpu as pltpu
from jax.sharding import PartitionSpec as P

F32 = jnp.float32
BF16 = jnp.bfloat16
NI = 1024
FACE = 256
R = 128
NX = 32
NY = 16
SL = R // NY
NCG = 1024
VMEM_BYTES = 60 * 1024 * 1024
PAD = 32
LONG = SL * 128 + 128
WIN = 32

ANY = pl.BlockSpec(memory_space=pl.ANY)
SMEM = pl.BlockSpec(memory_space=pltpu.SMEM)


class Taken:
    def __init__(self, source, buffer, semaphore):
        self.buffer = buffer
        self.copy = pltpu.make_async_copy(source, buffer, semaphore)
        self.copy.start()
        self.here = False

    def wait(self):
        if not self.here:
            self.copy.wait()
            self.here = True

    def __getitem__(self, index):
        self.wait()
        return self.buffer[index]

    def rows(self, first, size):
        self.wait()
        return self.buffer[pl.ds(pl.multiple_of(first, size), size)]


class Given:
    def __init__(self, target, buffer, semaphore):
        self.buffer = buffer
        self.copy = pltpu.make_async_copy(buffer, target, semaphore)
        self.sent = False

    def send(self):
        if not self.sent:
            self.copy.start()
            self.sent = True

    def __getitem__(self, index):
        return self.buffer[index]

    def __setitem__(self, index, value):
        self.buffer[index] = value


class Part(NamedTuple):
    array: jax.Array
    first: int
    size: int

    def shape(self):
        *blocks, _, width = self.array.shape
        return (*blocks, self.size, width)

    def of(self, ref):
        rows = pl.ds(self.first, self.size)
        return ref.at[rows] if self.array.ndim == 2 else ref.at[:, rows]


def call(kernel, args, outs, scratch=(), smem=0, flops=0):
    inputs = args[smem:]
    count = len(inputs)
    parts = [a if isinstance(a, Part) else None for a in inputs]
    args = [a.array if isinstance(a, Part) else a for a in args]
    size = sum(a.size * a.dtype.itemsize for a in args)
    shapes = [
        a.shape if part is None else part.shape() for a, part in zip(args[smem:], parts)
    ]
    whole = count + len(outs)

    def moved(*refs):
        scalars, refs = refs[:smem], refs[smem:]
        outside, buffers = refs[:whole], refs[whole : 2 * whole]
        semaphores, rest = refs[2 * whole], refs[2 * whole + 1 :]
        sources = [
            ref if part is None else part.of(ref) for ref, part in zip(outside, parts)
        ]
        taken = [Taken(sources[i], buffers[i], semaphores.at[i]) for i in range(count)]
        given = [Given(outside[i], buffers[i], semaphores.at[i]) for i in range(count, whole)]
        kernel(*scalars, *taken, *given, *rest)
        for value in given:
            value.send()
        for value in taken:
            value.wait()
        for value in given:
            value.copy.wait()

    return pl.pallas_call(
        moved,
        out_shape=tuple(jax.ShapeDtypeStruct(s, d) for s, d in outs),
        in_specs=[SMEM] * smem + [ANY] * count,
        out_specs=tuple(ANY for _ in outs),
        scratch_shapes=[pltpu.VMEM(t, a.dtype) for t, a in zip(shapes, args[smem:])]
        + [pltpu.VMEM(s, d) for s, d in outs]
        + [pltpu.SemaphoreType.DMA((whole,))]
        + list(scratch),
        compiler_params=pltpu.CompilerParams(vmem_limit_bytes=VMEM_BYTES),
        cost_estimate=pl.CostEstimate(flops=flops, bytes_accessed=size, transcendentals=0),
    )(*args)


def rows(i):
    return slice(FACE * i, FACE * (i + 1))


def dot(a, b):
    return jnp.dot(a, b, preferred_element_type=F32)


def lanes(shape):
    return lax.broadcasted_iota(jnp.int32, shape, len(shape) - 1)


def rolled(value, shift):
    shift = shift % 128
    return value if shift == 0 else pltpu.roll(value, shift, value.ndim - 1)


def total(value):
    return jnp.sum(value, axis=0, keepdims=True)


def place(out, base, column, piece, dx0, dy0):
    width = piece.shape[1]
    for cx in range(2):
        for cy in range(2):
            row = base + (dy0 + cy) * 8 + (dx0 + cx) * 2
            slot = 4 * cx + 2 * cy
            out[row : row + 2, column : column + width] = piece[slot : slot + 2]


def weights(ax, ay):
    shared = (ax[0] > 0, ax[0] < NX - 1, ay[0] > 0, ay[0] < NY - 1)
    return [jnp.where(face, 0.5, 1.0).astype(F32) for face in shared]


def thirds(value):
    high = value.astype(BF16).astype(F32)
    middle = (value - high).astype(BF16).astype(F32)
    return high, middle, value - high - middle


def start_kernel(ax, ay, ids, load, basis, inverse, coarse, l_out, msg_out, table, own):
    wt = weights(ax, ay)
    piece = coarse.rows(32 * (ax[0] % 2), 32)
    for k in range(8):
        column = piece[:, 128 * k : 128 * (k + 1)]
        msg_out[:, 32 * k : 32 * (k + 1)] = jnp.broadcast_to(column[None], (NY, 32, 128))
    scaled = [(load[rows(i)].astype(F32) * wt[i]).astype(BF16) for i in range(4)]
    scaled = jnp.concatenate(scaled, axis=0)
    own[...] = jnp.zeros((WIN, NI), F32)
    place(own, 0, 0, basis[...].astype(F32), 1, 1)
    table[...] = jnp.zeros((128, 128), F32)
    table[0:WIN] = dot(own[...].astype(BF16), scaled)
    for c in range(2):
        table[64 + c : 65 + c] = jnp.full((1, 128), ids[c].astype(F32))
    terms = thirds(jnp.transpose(table[...]).reshape(NY, SL, 128))
    terms = jnp.concatenate([*terms, jnp.zeros((NY, SL, 128), F32)], axis=1)
    msg_out[:, FACE : FACE + 32] = terms.astype(BF16)
    msg_out.send()
    for i in range(4):
        l_out[rows(i)] = wt[i] * dot(inverse[rows(i)], scaled)


def first_faces_kernel(l, basis, f0, f1, f2, f3):
    for i, face in enumerate((f0, f1, f2, f3)):
        face[0:FACE] = l[rows(i)]
        face[FACE : FACE + 8] = basis[:, FACE * i : FACE * i + 128].astype(F32)
        face[FACE + 8 : FACE + 16] = basis[:, FACE * i + 128 : FACE * (i + 1)].astype(F32)


def faces_kernel(s, f0, f1, f2, f3):
    for i, face in enumerate((f0, f1, f2, f3)):
        face[...] = s[rows(i)]
        face.send()


def window_kernel(basis, f0, f1, f2, f3, b_out, bt_out, table):
    table[...] = jnp.zeros((2 * WIN, NI), F32)
    place(table, 0, 0, basis[...].astype(F32), 1, 1)
    for i, (face, dx0, dy0) in enumerate(((f0, 0, 1), (f1, 2, 1), (f2, 1, 0), (f3, 1, 2))):
        for h in range(2):
            piece = face[FACE + 8 * h : FACE + 8 * h + 8]
            place(table, WIN, FACE * i + 128 * h, piece, dx0, dy0)
    b_out[...] = table[...].astype(BF16)
    bt_out[...] = jnp.transpose(table[...]).astype(BF16)


def local_kernel(ax, ay, s, f0, f1, f2, f3, inverse, q_out, l_out, g0, g1, g2, g3):
    wt = weights(ax, ay)
    parts = []
    for i, face in enumerate((f0, f1, f2, f3)):
        q = s[rows(i)].astype(F32) + face[...].astype(F32)
        q_out[rows(i)] = q
        parts.append((wt[i] * q).astype(BF16))
    q_out.send()
    scaled = jnp.concatenate(parts, axis=0)
    for i, face in enumerate((g0, g1, g2, g3)):
        local = wt[i] * dot(inverse[rows(i)], scaled)
        l_out[rows(i)] = local
        face[...] = local
        face.send()


def arrived(m):
    return jnp.transpose(m[...].reshape(R, 128))


def blended(wt, i, window_t, y, mine, facing):
    y = y[0:WIN].astype(BF16)
    mine = mine + wt[i] * dot(window_t[rows(i), 0:WIN], y)
    facing = facing + wt[i] * dot(window_t[rows(i), WIN:], y)
    return mine.astype(BF16).astype(F32) + facing.astype(BF16).astype(F32)


def split(value):
    high = value.astype(BF16)
    return jnp.concatenate([high, (value - high.astype(F32)).astype(BF16)], axis=1)


def joined(value):
    return value[:, 0:R] + value[:, R:]


def apply_schur(schur, zb, s_out, faces):
    for i in range(4):
        s = joined(dot(schur[rows(i)], zb[...]))
        s_out[rows(i)] = s
        if faces:
            faces[i][...] = s
            faces[i].send()
    s_out.send()


def window_terms(wt, window, s):
    terms = jnp.zeros((2 * WIN, 2 * R), F32)
    for i in range(4):
        terms += dot(window[:, rows(i)], split(s[rows(i)].astype(F32) * wt[i]))
    return joined(terms[0:WIN] + terms[WIN:])


def send_table(table, msg_out, terms, inner):
    table[...] = jnp.zeros((128, 128), F32)
    table[0:WIN] = terms
    for j, value in enumerate(inner):
        table[WIN + j : WIN + j + 1] = value
    msg_out[:, 0:SL] = jnp.transpose(table[...]).reshape(NY, SL, 128)
    msg_out[:, SL:] = jnp.zeros((NY, PAD - SL, 128), F32)


def first_kernel(
    ax, ay, m, window_t, l0, f0, f1, f2, f3, schur, window, load,
    z_out, s_out, g0, g1, g2, g3, msg_out, table, zb,
):
    wt = weights(ax, ay)
    y = arrived(m)
    for i, face in enumerate((f0, f1, f2, f3)):
        z = blended(wt, i, window_t, y, l0[rows(i)], face[0:FACE])
        z_out[rows(i)] = z
        zb[rows(i)] = z.astype(BF16)
    z_out.send()
    for i, face in enumerate((g0, g1, g2, g3)):
        s = dot(schur[rows(i)], zb[...]).astype(BF16)
        s_out[rows(i)] = s
        face[...] = s
        face.send()
    s_out.send()
    rz = jnp.zeros((1, R), F32)
    pq = jnp.zeros((1, R), F32)
    for i in range(4):
        z = z_out[rows(i)]
        rz += total(wt[i] * load[rows(i)].astype(F32) * z)
        pq += total(z * s_out[rows(i)].astype(F32))
    send_table(table, msg_out, window_terms(wt, window, s_out), (rz, pq))


def second_kernel(
    ax, ay, m, window_t, l0, e0, e1, e2, e3, l1, f0, f1, f2, f3, schur, window, q0, s0, load,
    z_out, s_out, g0, g1, g2, g3, msg_out, got_out, table, zb,
):
    wt = weights(ax, ay)
    got = arrived(m)
    got_out[...] = got[WIN : WIN + 8]
    alpha = got[WIN : WIN + 1]
    for i, (before, face) in enumerate(((e0, f0), (e1, f1), (e2, f2), (e3, f3))):
        mine = l0[rows(i)] - alpha * l1[rows(i)]
        facing = before[0:FACE] - alpha * face[...]
        z = blended(wt, i, window_t, got, mine, facing)
        z_out[rows(i)] = z
        zb[rows(i)] = split(z)
    z_out.send()
    apply_schur(schur, zb, s_out, (g0, g1, g2, g3))
    rz = jnp.zeros((1, R), F32)
    zz = jnp.zeros((1, R), F32)
    zq = jnp.zeros((1, R), F32)
    for i in range(4):
        z = z_out[rows(i)]
        r = load[rows(i)].astype(F32) - alpha * q0[rows(i)]
        rz += total(wt[i] * r * z)
        zz += total(z * s_out[rows(i)])
        zq += total(z * s0[rows(i)].astype(F32))
    send_table(table, msg_out, window_terms(wt, window, s_out), (rz, zz, zq))


def third_kernel(
    ax, ay, m, got0, window_t, l0, d0, d1, d2, d3, l1, e0, e1, e2, e3, l2, f0, f1, f2, f3,
    schur, q0, q1, s0, s1, load,
    z_out, s_out, msg_out, got_out, zb,
):
    wt = weights(ax, ay)
    got = arrived(m)
    got_out[...] = got[WIN : WIN + 8]
    alpha0 = got0[0:1]
    alpha = got[WIN : WIN + 1]
    beta = got[WIN + 1 : WIN + 2]
    scale = alpha0 + alpha * beta
    faces = ((d0, e0, f0), (d1, e1, f1), (d2, e2, f2), (d3, e3, f3))
    for i, (before, first, second) in enumerate(faces):
        mine = l0[rows(i)] - scale * l1[rows(i)] - alpha * l2[rows(i)]
        facing = before[0:FACE] - scale * first[...] - alpha * second[...]
        z = blended(wt, i, window_t, got, mine, facing)
        z_out[rows(i)] = z
        zb[rows(i)] = split(z)
    z_out.send()
    apply_schur(schur, zb, s_out, ())
    rz = jnp.zeros((1, R), F32)
    zz = jnp.zeros((1, R), F32)
    zq = jnp.zeros((1, R), F32)
    for i in range(4):
        z = z_out[rows(i)]
        s = s1[rows(i)] + beta * s0[rows(i)].astype(F32)
        r = load[rows(i)].astype(F32) - scale * q0[rows(i)] - alpha * q1[rows(i)]
        rz += total(wt[i] * r * z)
        zz += total(z * s_out[rows(i)])
        zq += total(z * s)
    inner = jnp.concatenate([rz, zz, zq, jnp.zeros((5, R), F32)], axis=0)
    msg_out[...] = jnp.broadcast_to(inner[None], (NY, 8, R))


def update_kernel(got0, got1, z0, z1, q0, q1, load, x_out, p_out, q_out, r_out):
    alpha0 = got0[0:1]
    alpha = got1[0:1]
    beta = got1[1:2]
    for i in range(4):
        p = z1[rows(i)] + beta * z0[rows(i)]
        q = q1[rows(i)] + beta * q0[rows(i)]
        p_out[rows(i)] = p
        q_out[rows(i)] = q
        x_out[rows(i)] = alpha0 * z0[rows(i)] + alpha * p
        r_out[rows(i)] = load[rows(i)].astype(F32) - alpha0 * q0[rows(i)] - alpha * q


def last_kernel(m, got, s, f0, f1, f2, f3, z, p, q, x, r, x_out, r_out):
    inner = jnp.sum(m[...], axis=0)
    rz1 = got[2:3]
    pq1 = got[3:4]
    rz = inner[0:1]
    beta = rz / rz1
    pq = inner[1:2] + 2.0 * beta * inner[2:3] + beta * beta * pq1
    alpha = rz / pq
    for i, face in enumerate((f0, f1, f2, f3)):
        product = s[rows(i)] + face[...] + beta * q[rows(i)]
        direction = z[rows(i)] + beta * p[rows(i)]
        x_out[rows(i)] = (x[rows(i)] + alpha * direction).astype(BF16)
        r_out[rows(i)] = (r[rows(i)] - alpha * product).astype(BF16)


def send_column(out, column, other):
    for r in range(SL):
        out[:, :, 128 * r : 128 * (r + 1)] = jnp.broadcast_to(column[r : r + 1][None], (NX, 1, 128))
    out[:, :, 128 * SL :] = jnp.broadcast_to(other[None], (NX, 1, 128))


def column_kernel(m, out):
    where = lanes((SL, 128))
    column = jnp.zeros((SL, 128), F32)
    inner = jnp.zeros((SL, 128), F32)
    for b in range(NY):
        value = m[b]
        column += rolled(jnp.where(where < WIN, value, 0.0), 8 * (b - 1))
        inner += jnp.where((where >= WIN) & (where < WIN + 16), value, 0.0)
    other = jnp.zeros((1, 128), F32)
    for r in range(SL):
        other += rolled(inner[r : r + 1], 16 * r - WIN)
    send_column(out, column, other)


def first_column_kernel(m, out):
    where = lanes((SL, 128))
    column = jnp.zeros((SL, 128), F32)
    other = jnp.zeros((SL, 128), F32)
    for b in range(NY):
        value = m[b].astype(F32)
        value = value[0:SL] + value[SL : 2 * SL] + value[2 * SL : 3 * SL]
        column += rolled(jnp.where(where < WIN, value, 0.0), 8 * (b - 1))
        named = jnp.where((where >= 64) & (where < 66), value, 0.0)
        other += rolled(named, 8 * b - 64)
    send_column(out, column, other[0:1])


def unpacked(m, columns):
    for r in range(SL):
        columns[:, r : r + 1] = m[:, :, 128 * r : 128 * (r + 1)]


def vertex_sums(columns, group):
    place_of = lanes((SL, 128)) % 8 // 2
    result = jnp.zeros((SL, 128), F32)
    for k in range(4):
        value = jnp.zeros((SL, 128), F32)
        for j in range(4):
            value += rolled(columns[(4 * group + k - j + 1) % NX], 2 * (k - j))
        result += jnp.where(place_of == k, value, 0.0)
    return result


def reply(out, y, scalars):
    where = lanes((SL, 128))
    rest = jnp.zeros((SL, 128), F32)
    for j, value in enumerate(scalars):
        rest += jnp.where(where == WIN + j, value, 0.0)
    for b in range(NY):
        out[b] = jnp.where(where < WIN, rolled(y, -8 * (b - 1)), rest)


def solve(sums, table, out, scalars):
    y = dot(sums[...].astype(BF16), table[...])
    reply(out, y.astype(BF16).astype(F32), scalars)


def first_solve_kernel(ax, m, mine, other, sums, table, out, columns, picked, spread):
    unpacked(m, columns)
    for group in range(8):
        sums[:, 128 * group : 128 * (group + 1)] = vertex_sums(columns, group)
    own = jnp.zeros((1, 128), F32)
    for j in range(4):
        own += rolled(m[(ax[0] + j - 1 + NX) % NX, :, 128 * SL :], 2 * j)
    for i in range(4):
        number = lax.broadcasted_iota(jnp.int32, (FACE, 128), 0).astype(F32) + float(FACE * i)
        spread[rows(i), 0:128] = jnp.where(number == own, 1.0, 0.0).astype(BF16)
    for half, inverse in enumerate((mine, other)):
        value = jnp.zeros((NCG // 2, 128), F32)
        for k in range(8):
            block = inverse[:, 32 * k : 32 * (k + 1)].reshape(NCG // 2, 128)
            value += dot(block, spread[128 * k : 128 * (k + 1), 0:128])
        picked[NCG // 2 * half : NCG // 2 * (half + 1)] = value.astype(BF16)
    core = ax[0] % 2
    lane = lanes((128, 128))
    for group in range(8):
        named = jnp.zeros((1, 128), F32)
        for k in range(4):
            named += rolled(m[4 * group + k, :, 128 * SL :], 2 * k)
        named = jnp.transpose(jnp.broadcast_to(named, (128, 128))).astype(jnp.int32)
        far = jnp.where(((named >> 5) & 1) != core, NCG // 2, 0)
        named = ((named >> 6) << 5) + (named & 31) + far
        for part in range(8):
            spread[128 * group : 128 * (group + 1), 128 * part : 128 * (part + 1)] = jnp.where(
                named == lane + 128 * part, 1.0, 0.0
            ).astype(BF16)
    for i in range(4):
        table[rows(i)] = dot(spread[rows(i)], picked[...]).astype(BF16)
    solve(sums, table, out, ())


def inner_sums(m, count):
    inner = jnp.sum(m[:, :, 128 * SL :], axis=0)
    offset = lanes((SL, 128)) - 16 * lax.broadcasted_iota(jnp.int32, (SL, 128), 0)
    return [
        jnp.sum(jnp.where(offset == j, inner, 0.0), axis=1, keepdims=True) for j in range(count)
    ]


def second_solve_kernel(m, sums0, table, change, sums, kept, out, columns):
    rz, pq = inner_sums(m, 2)
    alpha = rz / pq
    unpacked(m, columns)
    for group in range(8):
        part = slice(128 * group, 128 * (group + 1))
        value = vertex_sums(columns, group)
        change[:, part] = value
        sums[:, part] = sums0[:, part] - alpha * value
    kept[...] = jnp.where(lanes((SL, 128)) == 0, rz, pq)
    solve(sums, table, out, (alpha,))


def third_solve_kernel(m, sums1, table, change0, kept, out, columns, sums):
    rz, zz, zq = inner_sums(m, 3)
    beta = rz / kept[:, 0:1]
    pq = zz + 2.0 * beta * zq + beta * beta * kept[:, 1:2]
    alpha = rz / pq
    unpacked(m, columns)
    for group in range(8):
        part = slice(128 * group, 128 * (group + 1))
        value = vertex_sums(columns, group) + beta * change0[:, part]
        sums[:, part] = sums1[:, part] - alpha * value
    solve(sums, table, out, (alpha, beta, rz, pq))


def last_column_kernel(m, out):
    out[...] = jnp.broadcast_to(jnp.sum(m[...], axis=0)[None], (NX, 8, R))


def across(faces):
    low_x, high_x, low_y, high_y = faces
    result = []
    for axis, size, low, high in (("gx", NX, low_x, high_x), ("gy", NY, low_y, high_y)):
        up = [(i, i + 1) for i in range(size - 1)]
        down = [(j, i) for i, j in up]
        result.append(lax.ppermute(high, axis, up))
        result.append(lax.ppermute(low, axis, down))
    return result


def swap(value, axis):
    return lax.all_to_all(value, axis, 0, 0, tiled=True)


def after(value, *others):
    return lax.optimization_barrier((value, *others))[0]


def body(load_cases, schur_blocks, local_inverse, coarse_basis, corner_ids, coarse_inverse):
    load = load_cases[0, 0]
    schur = schur_blocks[0, 0]
    inverse = local_inverse[0, 0]
    basis = coarse_basis[0, 0]
    ids = corner_ids[0, 0]
    here = [lax.axis_index(axis).astype(jnp.int32).reshape(1) for axis in ("gx", "gy")]

    tall = (NI, R)
    msg = ((NY, SL, 128), F32)
    wide = ((NX, 1, LONG), F32)
    columns = pltpu.VMEM((NX, SL, 128), F32)
    block = 2 * NI * NI * R
    table = pltpu.VMEM((128, 128), F32)
    zb = pltpu.VMEM((NI, 2 * R), BF16)
    face = ((FACE, R), F32)

    l0, m = call(
        start_kernel,
        (*here, ids, load, basis, inverse, coarse_inverse),
        [(tall, F32), ((NY, FACE + 32, 128), BF16)],
        [table, pltpu.VMEM((WIN, NI), F32)],
        smem=3,
        flops=block,
    )
    f0, f1, f2, f3 = call(
        first_faces_kernel,
        (l0, basis),
        [((FACE + 16, R), F32)] * 4,
        flops=block,
    )
    faces0 = across((f0, f1, f2, f3))
    mine, *faces0 = lax.optimization_barrier((swap(m, "gy"), *faces0))
    other = lax.ppermute(mine, "gx", [(i, i ^ 1) for i in range(NX)])
    (m,) = call(first_column_kernel, (Part(mine, FACE, 32),), [wide])
    m = swap(m, "gx")
    window, window_t = call(
        window_kernel,
        (basis, *faces0),
        [((2 * WIN, NI), BF16), ((NI, 2 * WIN), BF16)],
        [pltpu.VMEM((2 * WIN, NI), F32)],
    )
    sums0, picked, m = call(
        first_solve_kernel,
        (here[0], after(m, window), Part(mine, 0, FACE), Part(other, 0, FACE)),
        [((SL, NCG), F32), ((NCG, 128), BF16), msg],
        [columns, pltpu.VMEM((NCG, 128), BF16), pltpu.VMEM((NCG, NCG), BF16)],
        smem=1,
        flops=2 * block,
    )
    m = swap(m, "gy")
    z0, s0, g0, g1, g2, g3, m = call(
        first_kernel,
        (*here, m, window_t, l0, *faces0, schur, window, load),
        [(tall, F32), (tall, BF16)] + [((FACE, R), BF16)] * 4 + [((NY, PAD, 128), F32)],
        [table, pltpu.VMEM(tall, BF16)],
        smem=2,
        flops=block,
    )

    def stage(s, faces, m):
        m, *faces = lax.optimization_barrier((swap(m, "gy"), *across(faces)))
        (m,) = call(column_kernel, (Part(m, 0, SL),), [wide])
        q, l, *faces = call(
            local_kernel,
            (*here, s, *faces, inverse),
            [(tall, F32), (tall, F32)] + [face] * 4,
            smem=2,
            flops=block,
        )
        m, *faces = lax.optimization_barrier((swap(m, "gx"), *across(faces)))
        return m, q, l, faces

    m, q0, l1, faces1 = stage(s0, (g0, g1, g2, g3), m)
    change0, sums1, kept, m = call(
        second_solve_kernel,
        (m, sums0, picked),
        [((SL, NCG), F32), ((SL, NCG), F32), ((SL, 128), F32), msg],
        [columns],
    )
    m = swap(m, "gy")
    z1, s1, g0, g1, g2, g3, m, got0 = call(
        second_kernel,
        (*here, m, window_t, l0, *faces0, l1, *faces1, schur, window, q0, s0, load),
        [(tall, F32), (tall, F32)] + [face] * 4 + [((NY, PAD, 128), F32), ((8, R), F32)],
        [table, zb],
        smem=2,
        flops=block,
    )

    m, q1, l2, faces2 = stage(s1, (g0, g1, g2, g3), m)
    (m,) = call(
        third_solve_kernel,
        (m, sums1, picked, change0, kept),
        [msg],
        [columns, pltpu.VMEM((SL, NCG), F32)],
    )
    m = swap(m, "gy")
    z2, s2, m, got1 = call(
        third_kernel,
        (
            *here, m, got0, window_t, l0, *faces0, l1, *faces1, l2, *faces2,
            schur, q0, q1, s0, s1, load,
        ),
        [(tall, F32), (tall, F32), ((NY, 8, R), F32), ((8, R), F32)],
        [zb],
        smem=2,
        flops=block,
    )

    m = swap(m, "gy")
    (sums,) = call(last_column_kernel, (m,), [((NX, 8, R), F32)])
    faces = across(call(faces_kernel, (after(s2, m),), [face] * 4, flops=block))
    x2, p1, q1, r2 = call(
        update_kernel,
        (got0, got1, after(z0, m), z1, q0, q1, load),
        [(tall, F32)] * 4,
        flops=block,
    )
    m = swap(sums, "gx")
    x, r = call(
        last_kernel,
        (m, got1, s2, *faces, z2, p1, q1, x2, r2),
        [(tall, BF16), (tall, BF16)],
    )
    return x[None, None], r[None, None]


def solution(mesh):
    return jax.shard_map(
        body,
        mesh=mesh,
        in_specs=(
            P("gx", "gy", None, None),
            P("gx", "gy", None, None),
            P("gx", "gy", None, None),
            P("gx", "gy", None, None),
            P("gx", "gy", None),
            P("gy", None),
        ),
        out_specs=(P("gx", "gy", None, None), P("gx", "gy", None, None)),
        check_vma=False,
    )
```

```python
from typing import NamedTuple

import jax
import jax.numpy as jnp
from jax import lax
from jax.experimental import pallas as pl
from jax.experimental.pallas import tpu as pltpu
from jax.sharding import PartitionSpec as P

F32 = jnp.float32
BF16 = jnp.bfloat16
NI = 1024
FACE = 256
R = 128
NX = 32
NY = 16
SL = R // NY
NCG = 1024
VMEM_BYTES = 60 * 1024 * 1024
SOME_BYTES = 16 * 1024 * 1024
PAD = 32
LONG = SL * 128 + 128
WIN = 32

ANY = pl.BlockSpec(memory_space=pl.ANY)
VMEM = pl.BlockSpec(memory_space=pltpu.VMEM)
SMEM = pl.BlockSpec(memory_space=pltpu.SMEM)


class Taken:
    def __init__(self, source, buffer, semaphore):
        self.buffer = buffer
        self.copy = pltpu.make_async_copy(source, buffer, semaphore)
        self.copy.start()
        self.here = False

    def wait(self):
        if not self.here:
            self.copy.wait()
            self.here = True

    def __getitem__(self, index):
        self.wait()
        return self.buffer[index]

    def rows(self, first, size):
        self.wait()
        return self.buffer[pl.ds(pl.multiple_of(first, size), size)]


class Given:
    def __init__(self, target, buffer, semaphore):
        self.buffer = buffer
        self.copy = pltpu.make_async_copy(buffer, target, semaphore)
        self.sent = False

    def send(self):
        if not self.sent:
            self.copy.start()
            self.sent = True

    def __getitem__(self, index):
        return self.buffer[index]

    def __setitem__(self, index, value):
        self.buffer[index] = value


class Part(NamedTuple):
    array: jax.Array
    first: int
    size: int

    def shape(self):
        *blocks, _, width = self.array.shape
        return (*blocks, self.size, width)

    def of(self, ref):
        rows = pl.ds(self.first, self.size)
        return ref.at[rows] if self.array.ndim == 2 else ref.at[:, rows]


class Near(NamedTuple):
    array: jax.Array


class Small(NamedTuple):
    shape: tuple
    dtype: jnp.dtype


def call(kernel, args, outs, scratch=(), smem=0, flops=0, limit=VMEM_BYTES):
    inputs = args[smem:]
    count = len(inputs)
    parts = [a if isinstance(a, Part) else None for a in inputs]
    near = [isinstance(a, Near) for a in inputs] + [isinstance(t, Small) for t in outs]
    args = [a.array if isinstance(a, (Part, Near)) else a for a in args]
    size = sum(a.size * a.dtype.itemsize for a in args)
    shapes = [
        a.shape if part is None else part.shape() for a, part in zip(args[smem:], parts)
    ]
    whole = count + len(outs)

    def moved(*refs):
        scalars, refs = refs[:smem], refs[smem:]
        outside, buffers = refs[:whole], refs[whole : 2 * whole]
        semaphores, rest = refs[2 * whole], refs[2 * whole + 1 :]
        sources = [
            ref if part is None else part.of(ref) for ref, part in zip(outside, parts)
        ]
        moving = [i for i in range(whole) if not near[i]]
        values = list(outside)
        for i in moving:
            if i < count:
                values[i] = Taken(sources[i], buffers[i], semaphores.at[i])
            else:
                values[i] = Given(outside[i], buffers[i], semaphores.at[i])
        kernel(*scalars, *values, *rest)
        for i in moving:
            if i >= count:
                values[i].send()
        for i in moving:
            if i < count:
                values[i].wait()
            else:
                values[i].copy.wait()

    return pl.pallas_call(
        moved,
        out_shape=tuple(jax.ShapeDtypeStruct(*t) for t in outs),
        in_specs=[SMEM] * smem + [VMEM if n else ANY for n in near[:count]],
        out_specs=tuple(VMEM if n else ANY for n in near[count:]),
        scratch_shapes=[
            pltpu.VMEM((8, 128) if n else t, a.dtype)
            for n, t, a in zip(near, shapes, args[smem:])
        ]
        + [pltpu.VMEM((8, 128) if n else t[0], t[1]) for n, t in zip(near[count:], outs)]
        + [pltpu.SemaphoreType.DMA((whole,))]
        + list(scratch),
        compiler_params=pltpu.CompilerParams(vmem_limit_bytes=limit),
        cost_estimate=pl.CostEstimate(flops=flops, bytes_accessed=size, transcendentals=0),
    )(*args)


def rows(i):
    return slice(FACE * i, FACE * (i + 1))


def dot(a, b):
    return jnp.dot(a, b, preferred_element_type=F32)


def lanes(shape):
    return lax.broadcasted_iota(jnp.int32, shape, len(shape) - 1)


def rolled(value, shift):
    shift = shift % 128
    return value if shift == 0 else pltpu.roll(value, shift, value.ndim - 1)


def total(value):
    return jnp.sum(value, axis=0, keepdims=True)


def place(out, base, column, piece, dx0, dy0):
    width = piece.shape[1]
    for cx in range(2):
        for cy in range(2):
            row = base + (dy0 + cy) * 8 + (dx0 + cx) * 2
            slot = 4 * cx + 2 * cy
            out[row : row + 2, column : column + width] = piece[slot : slot + 2]


def shared(ax, ay):
    return ax[0] > 0, ax[0] < NX - 1, ay[0] > 0, ay[0] < NY - 1


def weights(ax, ay):
    return [jnp.where(face, 0.5, 1.0).astype(F32) for face in shared(ax, ay)]


def facing(ax, ay, faces):
    return [
        jnp.where(there, face[0:FACE].astype(F32), 0.0)
        for there, face in zip(shared(ax, ay), faces)
    ]


def thirds(value):
    high = value.astype(BF16).astype(F32)
    middle = (value - high).astype(BF16).astype(F32)
    return high, middle, value - high - middle


def start_kernel(ax, ay, ids, load, basis, inverse, coarse, l_out, msg_out, table, own):
    wt = weights(ax, ay)
    piece = coarse.rows(32 * (ax[0] % 2), 32)
    for k in range(8):
        column = piece[:, 128 * k : 128 * (k + 1)]
        msg_out[:, 32 * k : 32 * (k + 1)] = jnp.broadcast_to(column[None], (NY, 32, 128))
    scaled = [(load[rows(i)].astype(F32) * wt[i]).astype(BF16) for i in range(4)]
    scaled = jnp.concatenate(scaled, axis=0)
    own[...] = jnp.zeros((WIN, NI), F32)
    place(own, 0, 0, basis[...].astype(F32), 1, 1)
    table[...] = jnp.zeros((128, 128), F32)
    table[0:WIN] = dot(own[...].astype(BF16), scaled)
    for c in range(2):
        table[64 + c : 65 + c] = jnp.full((1, 128), ids[c].astype(F32))
    terms = thirds(jnp.transpose(table[...]).reshape(NY, SL, 128))
    terms = jnp.concatenate([*terms, jnp.zeros((NY, SL, 128), F32)], axis=1)
    msg_out[:, FACE : FACE + 32] = terms.astype(BF16)
    msg_out.send()
    for i in range(4):
        l_out[rows(i)] = wt[i] * dot(inverse[rows(i)], scaled)


def first_faces_kernel(l, basis, f0, f1, f2, f3):
    for i, face in enumerate((f0, f1, f2, f3)):
        face[0:FACE] = l[rows(i)]
        face[FACE : FACE + 8] = basis[:, FACE * i : FACE * i + 128].astype(F32)
        face[FACE + 8 : FACE + 16] = basis[:, FACE * i + 128 : FACE * (i + 1)].astype(F32)


def window_kernel(ax, ay, basis, f0, f1, f2, f3, b_out, bt_out, table):
    table[...] = jnp.zeros((2 * WIN, NI), F32)
    place(table, 0, 0, basis[...].astype(F32), 1, 1)
    there = shared(ax, ay)
    for i, (face, dx0, dy0) in enumerate(((f0, 0, 1), (f1, 2, 1), (f2, 1, 0), (f3, 1, 2))):
        for h in range(2):
            piece = jnp.where(there[i], face[FACE + 8 * h : FACE + 8 * h + 8], 0.0)
            place(table, WIN, FACE * i + 128 * h, piece, dx0, dy0)
    b_out[...] = table[...].astype(BF16)
    bt_out[...] = jnp.transpose(table[...]).astype(BF16)


def local_kernel(ax, ay, s, f0, f1, f2, f3, inverse, q_out, l_out, g0, g1, g2, g3):
    wt = weights(ax, ay)
    parts = []
    for i, face in enumerate(facing(ax, ay, (f0, f1, f2, f3))):
        q = s[rows(i)].astype(F32) + face
        q_out[rows(i)] = q
        parts.append((wt[i] * q).astype(BF16))
    q_out.send()
    scaled = jnp.concatenate(parts, axis=0)
    for i, face in enumerate((g0, g1, g2, g3)):
        local = wt[i] * dot(inverse[rows(i)], scaled)
        l_out[rows(i)] = local
        face[...] = local
        face.send()


def arrived(m):
    return jnp.transpose(m[...].reshape(R, 128))


def blended(wt, i, window_t, y, mine, other):
    y = y[0:WIN].astype(BF16)
    mine = mine + wt[i] * dot(window_t[rows(i), 0:WIN], y)
    other = other + wt[i] * dot(window_t[rows(i), WIN:], y)
    return mine.astype(BF16).astype(F32) + other.astype(BF16).astype(F32)


def split(value):
    high = value.astype(BF16)
    return jnp.concatenate([high, (value - high.astype(F32)).astype(BF16)], axis=1)


def joined(value):
    return value[:, 0:R] + value[:, R:]


def apply_schur(schur, zb, s_out, faces):
    for i in range(4):
        s = joined(dot(schur[rows(i)], zb[...]))
        s_out[rows(i)] = s
        if faces:
            faces[i][...] = s
            faces[i].send()
    s_out.send()


def window_terms(wt, window, s):
    terms = jnp.zeros((2 * WIN, 2 * R), F32)
    for i in range(4):
        terms += dot(window[:, rows(i)], split(s[rows(i)].astype(F32) * wt[i]))
    return joined(terms[0:WIN] + terms[WIN:])


def send_table(table, msg_out, terms, inner):
    table[...] = jnp.zeros((128, 128), F32)
    table[0:WIN] = terms
    for j, value in enumerate(inner):
        table[WIN + j : WIN + j + 1] = value
    msg_out[:, 0:SL] = jnp.transpose(table[...]).reshape(NY, SL, 128)
    msg_out[:, SL:] = jnp.zeros((NY, PAD - SL, 128), F32)


def first_kernel(
    ax, ay, m, window_t, l0, f0, f1, f2, f3, schur, window, load,
    z_out, s_out, g0, g1, g2, g3, msg_out, table, zb,
):
    wt = weights(ax, ay)
    y = arrived(m)
    for i, face in enumerate(facing(ax, ay, (f0, f1, f2, f3))):
        z = blended(wt, i, window_t, y, l0[rows(i)], face)
        z_out[rows(i)] = z
        zb[rows(i)] = z.astype(BF16)
    z_out.send()
    for i, face in enumerate((g0, g1, g2, g3)):
        s = dot(schur[rows(i)], zb[...]).astype(BF16)
        s_out[rows(i)] = s
        face[...] = s
        face.send()
    s_out.send()
    rz = jnp.zeros((1, R), F32)
    pq = jnp.zeros((1, R), F32)
    for i in range(4):
        z = z_out[rows(i)]
        rz += total(wt[i] * load[rows(i)].astype(F32) * z)
        pq += total(z * s_out[rows(i)].astype(F32))
    send_table(table, msg_out, window_terms(wt, window, s_out), (rz, pq))


def second_kernel(
    ax, ay, m, window_t, l0, e0, e1, e2, e3, l1, f0, f1, f2, f3, schur, window, q0, s0, load,
    z_out, s_out, g0, g1, g2, g3, msg_out, got_out, table, zb,
):
    wt = weights(ax, ay)
    got = arrived(m)
    got_out[...] = got[WIN : WIN + 8]
    alpha = got[WIN : WIN + 1]
    before = facing(ax, ay, (e0, e1, e2, e3))
    first = facing(ax, ay, (f0, f1, f2, f3))
    for i in range(4):
        mine = l0[rows(i)] - alpha * l1[rows(i)]
        z = blended(wt, i, window_t, got, mine, before[i] - alpha * first[i])
        z_out[rows(i)] = z
        zb[rows(i)] = split(z)
    z_out.send()
    apply_schur(schur, zb, s_out, (g0, g1, g2, g3))
    rz = jnp.zeros((1, R), F32)
    zz = jnp.zeros((1, R), F32)
    zq = jnp.zeros((1, R), F32)
    for i in range(4):
        z = z_out[rows(i)]
        r = load[rows(i)].astype(F32) - alpha * q0[rows(i)]
        rz += total(wt[i] * r * z)
        zz += total(z * s_out[rows(i)])
        zq += total(z * s0[rows(i)].astype(F32))
    send_table(table, msg_out, window_terms(wt, window, s_out), (rz, zz, zq))


def third_kernel(
    ax, ay, m, got0, window_t, l0, d0, d1, d2, d3, l1, e0, e1, e2, e3, l2, f0, f1, f2, f3,
    schur, q0, q1, s0, s1, load,
    z_out, s_out, g0, g1, g2, g3, msg_out, got_out, zb,
):
    wt = weights(ax, ay)
    got = arrived(m)
    got_out[...] = got[WIN : WIN + 8]
    alpha0 = got0[0:1]
    alpha = got[WIN : WIN + 1]
    beta = got[WIN + 1 : WIN + 2]
    scale = alpha0 + alpha * beta
    before = facing(ax, ay, (d0, d1, d2, d3))
    first = facing(ax, ay, (e0, e1, e2, e3))
    second = facing(ax, ay, (f0, f1, f2, f3))
    for i in range(4):
        mine = l0[rows(i)] - scale * l1[rows(i)] - alpha * l2[rows(i)]
        other = before[i] - scale * first[i] - alpha * second[i]
        z = blended(wt, i, window_t, got, mine, other)
        z_out[rows(i)] = z
        zb[rows(i)] = split(z)
    z_out.send()
    apply_schur(schur, zb, s_out, (g0, g1, g2, g3))
    rz = jnp.zeros((1, R), F32)
    zz = jnp.zeros((1, R), F32)
    zq = jnp.zeros((1, R), F32)
    for i in range(4):
        z = z_out[rows(i)]
        s = s1[rows(i)] + beta * s0[rows(i)].astype(F32)
        r = load[rows(i)].astype(F32) - scale * q0[rows(i)] - alpha * q1[rows(i)]
        rz += total(wt[i] * r * z)
        zz += total(z * s_out[rows(i)])
        zq += total(z * s)
    inner = jnp.concatenate([rz, zz, zq, jnp.zeros((PAD - 3, R), F32)], axis=0)
    msg_out[...] = jnp.broadcast_to(inner[None], (NY, PAD, R))


def update_kernel(got0, got1, z0, z1, q0, q1, load, x_out, p_out, q_out, r_out):
    alpha0 = got0[0:1]
    alpha = got1[0:1]
    beta = got1[1:2]
    for i in range(4):
        p = z1[rows(i)] + beta * z0[rows(i)]
        q = q1[rows(i)] + beta * q0[rows(i)]
        p_out[rows(i)] = p
        q_out[rows(i)] = q
        x_out[rows(i)] = alpha0 * z0[rows(i)] + alpha * p
        r_out[rows(i)] = load[rows(i)].astype(F32) - alpha0 * q0[rows(i)] - alpha * q


def last_kernel(ax, ay, m, got, s, f0, f1, f2, f3, z, p, q, x, r, x_out, r_out):
    inner = jnp.sum(m[...], axis=0)
    rz1 = got[2:3]
    pq1 = got[3:4]
    rz = inner[0:1]
    beta = rz / rz1
    pq = inner[1:2] + 2.0 * beta * inner[2:3] + beta * beta * pq1
    alpha = rz / pq
    for i, face in enumerate(facing(ax, ay, (f0, f1, f2, f3))):
        product = s[rows(i)] + face + beta * q[rows(i)]
        direction = z[rows(i)] + beta * p[rows(i)]
        x_out[rows(i)] = (x[rows(i)] + alpha * direction).astype(BF16)
        r_out[rows(i)] = (r[rows(i)] - alpha * product).astype(BF16)


def send_column(out, column, other):
    for r in range(SL):
        out[:, :, 128 * r : 128 * (r + 1)] = jnp.broadcast_to(column[r : r + 1][None], (NX, 1, 128))
    out[:, :, 128 * SL :] = jnp.broadcast_to(other[None], (NX, 1, 128))


def column_kernel(m, out):
    where = lanes((SL, 128))
    column = jnp.zeros((SL, 128), F32)
    inner = jnp.zeros((SL, 128), F32)
    for b in range(NY):
        value = m[b]
        column += rolled(jnp.where(where < WIN, value, 0.0), 8 * (b - 1))
        inner += jnp.where((where >= WIN) & (where < WIN + 16), value, 0.0)
    other = jnp.zeros((1, 128), F32)
    for r in range(SL):
        other += rolled(inner[r : r + 1], 16 * r - WIN)
    send_column(out, column, other)


def first_column_kernel(m, out):
    where = lanes((SL, 128))
    column = jnp.zeros((SL, 128), F32)
    other = jnp.zeros((SL, 128), F32)
    for b in range(NY):
        value = m[b].astype(F32)
        value = value[0:SL] + value[SL : 2 * SL] + value[2 * SL : 3 * SL]
        column += rolled(jnp.where(where < WIN, value, 0.0), 8 * (b - 1))
        named = jnp.where((where >= 64) & (where < 66), value, 0.0)
        other += rolled(named, 8 * b - 64)
    send_column(out, column, other[0:1])


def unpacked(m, columns):
    for r in range(SL):
        columns[:, r : r + 1] = m[:, :, 128 * r : 128 * (r + 1)]


def vertex_sums(columns, group):
    place_of = lanes((SL, 128)) % 8 // 2
    result = jnp.zeros((SL, 128), F32)
    for k in range(4):
        value = jnp.zeros((SL, 128), F32)
        for j in range(4):
            value += rolled(columns[(4 * group + k - j + 1) % NX], 2 * (k - j))
        result += jnp.where(place_of == k, value, 0.0)
    return result


def reply(out, y, scalars):
    where = lanes((SL, 128))
    rest = jnp.zeros((SL, 128), F32)
    for j, value in enumerate(scalars):
        rest += jnp.where(where == WIN + j, value, 0.0)
    for b in range(NY):
        out[b] = jnp.where(where < WIN, rolled(y, -8 * (b - 1)), rest)


def solve(sums, table, out, scalars):
    y = dot(sums[...].astype(BF16), table[...])
    reply(out, y.astype(BF16).astype(F32), scalars)


def first_solve_kernel(ax, m, mine, other, sums, table, out, columns, picked, spread):
    unpacked(m, columns)
    for group in range(8):
        sums[:, 128 * group : 128 * (group + 1)] = vertex_sums(columns, group)
    own = jnp.zeros((1, 128), F32)
    for j in range(4):
        own += rolled(m[(ax[0] + j - 1 + NX) % NX, :, 128 * SL :], 2 * j)
    for i in range(4):
        number = lax.broadcasted_iota(jnp.int32, (FACE, 128), 0).astype(F32) + float(FACE * i)
        spread[rows(i), 0:128] = jnp.where(number == own, 1.0, 0.0).astype(BF16)
    for half, inverse in enumerate((mine, other)):
        value = jnp.zeros((NCG // 2, 128), F32)
        for k in range(8):
            block = inverse[:, 32 * k : 32 * (k + 1)].reshape(NCG // 2, 128)
            value += dot(block, spread[128 * k : 128 * (k + 1), 0:128])
        picked[NCG // 2 * half : NCG // 2 * (half + 1)] = value.astype(BF16)
    core = ax[0] % 2
    lane = lanes((128, 128))
    for group in range(8):
        named = jnp.zeros((1, 128), F32)
        for k in range(4):
            named += rolled(m[4 * group + k, :, 128 * SL :], 2 * k)
        named = jnp.transpose(jnp.broadcast_to(named, (128, 128))).astype(jnp.int32)
        far = jnp.where(((named >> 5) & 1) != core, NCG // 2, 0)
        named = ((named >> 6) << 5) + (named & 31) + far
        for part in range(8):
            spread[128 * group : 128 * (group + 1), 128 * part : 128 * (part + 1)] = jnp.where(
                named == lane + 128 * part, 1.0, 0.0
            ).astype(BF16)
    for i in range(4):
        table[rows(i)] = dot(spread[rows(i)], picked[...]).astype(BF16)
    solve(sums, table, out, ())


def inner_sums(m, count):
    inner = jnp.sum(m[:, :, 128 * SL :], axis=0)
    offset = lanes((SL, 128)) - 16 * lax.broadcasted_iota(jnp.int32, (SL, 128), 0)
    return [
        jnp.sum(jnp.where(offset == j, inner, 0.0), axis=1, keepdims=True) for j in range(count)
    ]


def second_solve_kernel(m, sums0, table, change, sums, kept, out, columns):
    rz, pq = inner_sums(m, 2)
    alpha = rz / pq
    unpacked(m, columns)
    for group in range(8):
        part = slice(128 * group, 128 * (group + 1))
        value = vertex_sums(columns, group)
        change[:, part] = value
        sums[:, part] = sums0[:, part] - alpha * value
    kept[...] = jnp.where(lanes((SL, 128)) == 0, rz, pq)
    solve(sums, table, out, (alpha,))


def third_solve_kernel(m, sums1, table, change0, kept, out, columns, sums):
    rz, zz, zq = inner_sums(m, 3)
    beta = rz / kept[:, 0:1]
    pq = zz + 2.0 * beta * zq + beta * beta * kept[:, 1:2]
    alpha = rz / pq
    unpacked(m, columns)
    for group in range(8):
        part = slice(128 * group, 128 * (group + 1))
        value = vertex_sums(columns, group) + beta * change0[:, part]
        sums[:, part] = sums1[:, part] - alpha * value
    solve(sums, table, out, (alpha, beta, rz, pq))


def last_column_kernel(m, out):
    out[...] = jnp.broadcast_to(jnp.sum(m[...], axis=0)[None], (NX, 8, R))


def across(axis, low, high):
    size = {"gx": NX, "gy": NY}[axis]
    up = [(i, (i + 1) % size) for i in range(size)]
    down = [(j, i) for i, j in up]
    return lax.ppermute(high, axis, up), lax.ppermute(low, axis, down)


def all_across(low_x, high_x, low_y, high_y):
    y = across("gy", low_y, high_y)
    return *across("gx", low_x, high_x), *y


def together(*values):
    return lax.optimization_barrier(values)


def swap(value, axis):
    return lax.all_to_all(value, axis, 0, 0, tiled=True)


def body(load_cases, schur_blocks, local_inverse, coarse_basis, corner_ids, coarse_inverse):
    load = load_cases[0, 0]
    schur = schur_blocks[0, 0]
    inverse = local_inverse[0, 0]
    basis = coarse_basis[0, 0]
    ids = corner_ids[0, 0]
    here = [lax.axis_index(axis).astype(jnp.int32).reshape(1) for axis in ("gx", "gy")]

    tall = (NI, R)
    msg = ((NY, SL, 128), F32)
    padded = ((NY, PAD, 128), F32)
    wide = ((NX, 1, LONG), F32)
    columns = pltpu.VMEM((NX, SL, 128), F32)
    block = 2 * NI * NI * R
    table = pltpu.VMEM((128, 128), F32)
    zb = pltpu.VMEM((NI, 2 * R), BF16)
    face = ((FACE, R), F32)

    l0, m = call(
        start_kernel,
        (*here, ids, load, basis, inverse, coarse_inverse),
        [(tall, F32), ((NY, FACE + 32, 128), BF16)],
        [table, pltpu.VMEM((WIN, NI), F32)],
        smem=3,
        flops=block,
    )
    f0, f1, f2, f3 = call(
        first_faces_kernel,
        (l0, basis),
        [((FACE + 16, R), F32)] * 4,
        flops=block,
    )
    faces0 = all_across(f0, f1, f2, f3)
    mine, *faces0 = together(swap(m, "gy"), *faces0)
    other = lax.ppermute(mine, "gx", [(i, i ^ 1) for i in range(NX)])
    (m,) = call(first_column_kernel, (Part(mine, FACE, 32),), [wide], limit=SOME_BYTES)
    m = swap(m, "gx")
    window, window_t = call(
        window_kernel,
        (*here, basis, *faces0),
        [((2 * WIN, NI), BF16), ((NI, 2 * WIN), BF16)],
        [pltpu.VMEM((2 * WIN, NI), F32)],
        smem=2,
    )
    sums0, picked, m = call(
        first_solve_kernel,
        (here[0], together(m, window)[0], Part(mine, 0, FACE), Part(other, 0, FACE)),
        [((SL, NCG), F32), ((NCG, 128), BF16), msg],
        [columns, pltpu.VMEM((NCG, 128), BF16), pltpu.VMEM((NCG, NCG), BF16)],
        smem=1,
        flops=2 * block,
    )
    m = swap(m, "gy")
    z0, s0, g0, g1, g2, g3, m = call(
        first_kernel,
        (*here, m, window_t, l0, *faces0, schur, window, load),
        [(tall, F32), (tall, BF16)] + [((FACE, R), BF16)] * 4 + [padded],
        [table, pltpu.VMEM(tall, BF16)],
        smem=2,
        flops=block,
    )

    def stage(s, faces, m):
        m, *faces = together(swap(m, "gy"), *all_across(*faces))
        (m,) = call(column_kernel, (Part(m, 0, SL),), [wide], limit=SOME_BYTES)
        q, l, *faces = call(
            local_kernel,
            (*here, s, *faces, inverse),
            [(tall, F32), (tall, F32)] + [face] * 4,
            smem=2,
            flops=block,
        )
        m, *faces = together(swap(m, "gx"), *all_across(*faces))
        return m, q, l, faces

    m, q0, l1, faces1 = stage(s0, (g0, g1, g2, g3), m)
    change0, sums1, kept, m = call(
        second_solve_kernel,
        (Near(m), sums0, picked),
        [((SL, NCG), F32), ((SL, NCG), F32), ((SL, 128), F32), msg],
        [columns],
        limit=SOME_BYTES,
    )
    m = swap(m, "gy")
    z1, s1, g0, g1, g2, g3, m, got0 = call(
        second_kernel,
        (*here, m, window_t, l0, *faces0, l1, *faces1, schur, window, q0, s0, load),
        [(tall, F32), (tall, F32)] + [face] * 4 + [padded, ((8, R), F32)],
        [table, zb],
        smem=2,
        flops=block,
    )

    m, q1, l2, faces2 = stage(s1, (g0, g1, g2, g3), m)
    (m,) = call(
        third_solve_kernel,
        (Near(m), sums1, picked, change0, kept),
        [msg],
        [columns, pltpu.VMEM((SL, NCG), F32)],
        limit=SOME_BYTES,
    )
    m = swap(m, "gy")
    z2, s2, g0, g1, g2, g3, m, got1 = call(
        third_kernel,
        (
            *here, m, got0, window_t, l0, *faces0, l1, *faces1, l2, *faces2,
            schur, q0, q1, s0, s1, load,
        ),
        [(tall, F32), (tall, F32)] + [face] * 4 + [padded, ((8, R), F32)],
        [zb],
        smem=2,
        flops=block,
    )

    m, *faces, g2, g3, z0 = together(swap(m, "gy"), *across("gx", g0, g1), g2, g3, z0)
    (sums,) = call(last_column_kernel, (Part(m, 0, SL),), [((NX, 8, R), F32)], limit=SOME_BYTES)
    faces += across("gy", g2, g3)
    x2, p1, q1, r2 = call(
        update_kernel,
        (got0, got1, z0, z1, q0, q1, load),
        [(tall, F32)] * 4,
        flops=block,
    )
    m = swap(sums, "gx")
    x, r = call(
        last_kernel,
        (*here, m, got1, s2, *faces, z2, p1, q1, x2, r2),
        [(tall, BF16), (tall, BF16)],
        smem=2,
    )
    return x[None, None], r[None, None]


def solution(mesh):
    return jax.shard_map(
        body,
        mesh=mesh,
        in_specs=(
            P("gx", "gy", None, None),
            P("gx", "gy", None, None),
            P("gx", "gy", None, None),
            P("gx", "gy", None, None),
            P("gx", "gy", None),
            P("gy", None),
        ),
        out_specs=(P("gx", "gy", None, None), P("gx", "gy", None, None)),
        check_vma=False,
    )
```

```python
from typing import NamedTuple

import jax
import jax.numpy as jnp
from jax import lax
from jax.experimental import pallas as pl
from jax.experimental.pallas import tpu as pltpu
from jax.sharding import PartitionSpec as P

F32 = jnp.float32
BF16 = jnp.bfloat16
NI = 1024
FACE = 256
R = 128
NX = 32
NY = 16
SL = R // NY
NCG = 1024
VMEM_BYTES = 60 * 1024 * 1024
SOME_BYTES = 16 * 1024 * 1024
PAD = 32
LONG = SL * 128 + 128
WIN = 32

ANY = pl.BlockSpec(memory_space=pl.ANY)
VMEM = pl.BlockSpec(memory_space=pltpu.VMEM)
SMEM = pl.BlockSpec(memory_space=pltpu.SMEM)


class Taken:
    def __init__(self, source, buffer, semaphore):
        self.buffer = buffer
        self.copy = pltpu.make_async_copy(source, buffer, semaphore)
        self.copy.start()
        self.here = False

    def wait(self):
        if not self.here:
            self.copy.wait()
            self.here = True

    def __getitem__(self, index):
        self.wait()
        return self.buffer[index]

    def rows(self, first, size):
        self.wait()
        return self.buffer[pl.ds(pl.multiple_of(first, size), size)]


class Given:
    def __init__(self, target, buffer, semaphore):
        self.buffer = buffer
        self.copy = pltpu.make_async_copy(buffer, target, semaphore)
        self.sent = False

    def send(self):
        if not self.sent:
            self.copy.start()
            self.sent = True

    def __getitem__(self, index):
        return self.buffer[index]

    def __setitem__(self, index, value):
        self.buffer[index] = value


class Part(NamedTuple):
    array: jax.Array
    first: int
    size: int

    def shape(self):
        *blocks, _, width = self.array.shape
        return (*blocks, self.size, width)

    def of(self, ref):
        rows = pl.ds(self.first, self.size)
        return ref.at[rows] if self.array.ndim == 2 else ref.at[:, rows]


class Near(NamedTuple):
    array: jax.Array


class Small(NamedTuple):
    shape: tuple
    dtype: jnp.dtype


def call(kernel, args, outs, scratch=(), smem=0, flops=0, limit=VMEM_BYTES):
    inputs = args[smem:]
    count = len(inputs)
    parts = [a if isinstance(a, Part) else None for a in inputs]
    near = [isinstance(a, Near) for a in inputs] + [isinstance(t, Small) for t in outs]
    args = [a.array if isinstance(a, (Part, Near)) else a for a in args]
    size = sum(a.size * a.dtype.itemsize for a in args)
    shapes = [
        a.shape if part is None else part.shape() for a, part in zip(args[smem:], parts)
    ]
    whole = count + len(outs)

    def moved(*refs):
        scalars, refs = refs[:smem], refs[smem:]
        outside, buffers = refs[:whole], refs[whole : 2 * whole]
        semaphores, rest = refs[2 * whole], refs[2 * whole + 1 :]
        sources = [
            ref if part is None else part.of(ref) for ref, part in zip(outside, parts)
        ]
        moving = [i for i in range(whole) if not near[i]]
        values = list(outside)
        for i in moving:
            if i < count:
                values[i] = Taken(sources[i], buffers[i], semaphores.at[i])
            else:
                values[i] = Given(outside[i], buffers[i], semaphores.at[i])
        kernel(*scalars, *values, *rest)
        for i in moving:
            if i >= count:
                values[i].send()
        for i in moving:
            if i < count:
                values[i].wait()
            else:
                values[i].copy.wait()

    return pl.pallas_call(
        moved,
        out_shape=tuple(jax.ShapeDtypeStruct(*t) for t in outs),
        in_specs=[SMEM] * smem + [VMEM if n else ANY for n in near[:count]],
        out_specs=tuple(VMEM if n else ANY for n in near[count:]),
        scratch_shapes=[
            pltpu.VMEM((8, 128) if n else t, a.dtype)
            for n, t, a in zip(near, shapes, args[smem:])
        ]
        + [pltpu.VMEM((8, 128) if n else t[0], t[1]) for n, t in zip(near[count:], outs)]
        + [pltpu.SemaphoreType.DMA((whole,))]
        + list(scratch),
        compiler_params=pltpu.CompilerParams(vmem_limit_bytes=limit),
        cost_estimate=pl.CostEstimate(flops=flops, bytes_accessed=size, transcendentals=0),
    )(*args)


def rows(i):
    return slice(FACE * i, FACE * (i + 1))


def dot(a, b):
    return jnp.dot(a, b, preferred_element_type=F32)


def lanes(shape):
    return lax.broadcasted_iota(jnp.int32, shape, len(shape) - 1)


def rolled(value, shift):
    shift = shift % 128
    return value if shift == 0 else pltpu.roll(value, shift, value.ndim - 1)


def total(value):
    return jnp.sum(value, axis=0, keepdims=True)


def place(out, base, column, piece, dx0, dy0):
    width = piece.shape[1]
    for cx in range(2):
        for cy in range(2):
            row = base + (dy0 + cy) * 8 + (dx0 + cx) * 2
            slot = 4 * cx + 2 * cy
            out[row : row + 2, column : column + width] = piece[slot : slot + 2]


def shared(ax, ay):
    return ax[0] > 0, ax[0] < NX - 1, ay[0] > 0, ay[0] < NY - 1


def weights(ax, ay):
    return [jnp.where(face, 0.5, 1.0).astype(F32) for face in shared(ax, ay)]


def facing(ax, ay, faces):
    return [
        jnp.where(there, face[0:FACE].astype(F32), 0.0)
        for there, face in zip(shared(ax, ay), faces)
    ]


def thirds(value):
    high = value.astype(BF16).astype(F32)
    middle = (value - high).astype(BF16).astype(F32)
    return high, middle, value - high - middle


def start_kernel(
    ax, ay, ids, load, basis, inverse, coarse, l_out, f0, f1, f2, f3, msg_out, table, own
):
    wt = weights(ax, ay)
    piece = coarse.rows(32 * (ax[0] % 2), 32)
    for k in range(8):
        column = piece[:, 128 * k : 128 * (k + 1)]
        msg_out[:, 32 * k : 32 * (k + 1)] = jnp.broadcast_to(column[None], (NY, 32, 128))
    scaled = [(load[rows(i)].astype(F32) * wt[i]).astype(BF16) for i in range(4)]
    scaled = jnp.concatenate(scaled, axis=0)
    own[...] = jnp.zeros((WIN, NI), F32)
    place(own, 0, 0, basis[...].astype(F32), 1, 1)
    table[...] = jnp.zeros((128, 128), F32)
    table[0:WIN] = dot(own[...].astype(BF16), scaled)
    for c in range(2):
        table[64 + c : 65 + c] = jnp.full((1, 128), ids[c].astype(F32))
    terms = thirds(jnp.transpose(table[...]).reshape(NY, SL, 128))
    terms = jnp.concatenate([*terms, jnp.zeros((NY, SL, 128), F32)], axis=1)
    msg_out[:, FACE : FACE + 32] = terms.astype(BF16)
    msg_out.send()
    for i, face in enumerate((f0, f1, f2, f3)):
        local = wt[i] * dot(inverse[rows(i)], scaled)
        l_out[rows(i)] = local
        face[0:FACE] = local
        face[FACE : FACE + 8] = basis[:, FACE * i : FACE * i + 128].astype(F32)
        face[FACE + 8 : FACE + 16] = basis[:, FACE * i + 128 : FACE * (i + 1)].astype(F32)
        face.send()


def window_kernel(ax, ay, basis, f0, f1, f2, f3, b_out, bt_out, table):
    table[...] = jnp.zeros((2 * WIN, NI), F32)
    place(table, 0, 0, basis[...].astype(F32), 1, 1)
    there = shared(ax, ay)
    for i, (face, dx0, dy0) in enumerate(((f0, 0, 1), (f1, 2, 1), (f2, 1, 0), (f3, 1, 2))):
        for h in range(2):
            piece = jnp.where(there[i], face[FACE + 8 * h : FACE + 8 * h + 8], 0.0)
            place(table, WIN, FACE * i + 128 * h, piece, dx0, dy0)
    b_out[...] = table[...].astype(BF16)
    bt_out[...] = jnp.transpose(table[...]).astype(BF16)


def local_kernel(ax, ay, s, f0, f1, f2, f3, inverse, q_out, l_out, g0, g1, g2, g3):
    wt = weights(ax, ay)
    parts = []
    for i, face in enumerate(facing(ax, ay, (f0, f1, f2, f3))):
        q = s[rows(i)].astype(F32) + face
        q_out[rows(i)] = q
        parts.append((wt[i] * q).astype(BF16))
    q_out.send()
    scaled = jnp.concatenate(parts, axis=0)
    for i, face in enumerate((g0, g1, g2, g3)):
        local = wt[i] * dot(inverse[rows(i)], scaled)
        l_out[rows(i)] = local
        face[...] = local
        face.send()


def arrived(m):
    return jnp.transpose(m[...].reshape(R, 128))


def blended(wt, i, window_t, y, mine, other):
    y = y[0:WIN].astype(BF16)
    mine = mine + wt[i] * dot(window_t[rows(i), 0:WIN], y)
    other = other + wt[i] * dot(window_t[rows(i), WIN:], y)
    return mine.astype(BF16).astype(F32) + other.astype(BF16).astype(F32)


def split(value):
    high = value.astype(BF16)
    return jnp.concatenate([high, (value - high.astype(F32)).astype(BF16)], axis=1)


def joined(value):
    return value[:, 0:R] + value[:, R:]


def apply_schur(schur, zb, s_out, faces):
    for i in range(4):
        s = joined(dot(schur[rows(i)], zb[...]))
        s_out[rows(i)] = s
        if faces:
            faces[i][...] = s
            faces[i].send()
    s_out.send()


def window_terms(wt, window, s):
    terms = jnp.zeros((2 * WIN, 2 * R), F32)
    for i in range(4):
        terms += dot(window[:, rows(i)], split(s[rows(i)].astype(F32) * wt[i]))
    return joined(terms[0:WIN] + terms[WIN:])


def send_table(table, msg_out, terms, inner):
    table[...] = jnp.zeros((128, 128), F32)
    table[0:WIN] = terms
    for j, value in enumerate(inner):
        table[WIN + j : WIN + j + 1] = value
    msg_out[:, 0:SL] = jnp.transpose(table[...]).reshape(NY, SL, 128)
    msg_out[:, SL:] = jnp.zeros((NY, PAD - SL, 128), F32)


def first_kernel(
    ax, ay, m, window_t, l0, f0, f1, f2, f3, schur, window, load,
    z_out, s_out, g0, g1, g2, g3, msg_out, table, zb,
):
    wt = weights(ax, ay)
    y = arrived(m)
    for i, face in enumerate(facing(ax, ay, (f0, f1, f2, f3))):
        z = blended(wt, i, window_t, y, l0[rows(i)], face)
        z_out[rows(i)] = z
        zb[rows(i)] = z.astype(BF16)
    z_out.send()
    for i, face in enumerate((g0, g1, g2, g3)):
        s = dot(schur[rows(i)], zb[...]).astype(BF16)
        s_out[rows(i)] = s
        face[...] = s
        face.send()
    s_out.send()
    rz = jnp.zeros((1, R), F32)
    pq = jnp.zeros((1, R), F32)
    for i in range(4):
        z = z_out[rows(i)]
        rz += total(wt[i] * load[rows(i)].astype(F32) * z)
        pq += total(z * s_out[rows(i)].astype(F32))
    send_table(table, msg_out, window_terms(wt, window, s_out), (rz, pq))


def second_kernel(
    ax, ay, m, window_t, l0, e0, e1, e2, e3, l1, f0, f1, f2, f3, schur, window, q0, s0, load,
    z_out, s_out, g0, g1, g2, g3, msg_out, got_out, table, zb,
):
    wt = weights(ax, ay)
    got = arrived(m)
    got_out[...] = got[WIN : WIN + 8]
    alpha = got[WIN : WIN + 1]
    before = facing(ax, ay, (e0, e1, e2, e3))
    first = facing(ax, ay, (f0, f1, f2, f3))
    for i in range(4):
        mine = l0[rows(i)] - alpha * l1[rows(i)]
        z = blended(wt, i, window_t, got, mine, before[i] - alpha * first[i])
        z_out[rows(i)] = z
        zb[rows(i)] = split(z)
    z_out.send()
    apply_schur(schur, zb, s_out, (g0, g1, g2, g3))
    rz = jnp.zeros((1, R), F32)
    zz = jnp.zeros((1, R), F32)
    zq = jnp.zeros((1, R), F32)
    for i in range(4):
        z = z_out[rows(i)]
        r = load[rows(i)].astype(F32) - alpha * q0[rows(i)]
        rz += total(wt[i] * r * z)
        zz += total(z * s_out[rows(i)])
        zq += total(z * s0[rows(i)].astype(F32))
    send_table(table, msg_out, window_terms(wt, window, s_out), (rz, zz, zq))


def third_kernel(
    ax, ay, m, got0, window_t, l0, d0, d1, d2, d3, l1, e0, e1, e2, e3, l2, f0, f1, f2, f3,
    schur, q0, q1, s0, s1, load,
    z_out, s_out, g0, g1, g2, g3, msg_out, got_out, zb,
):
    wt = weights(ax, ay)
    got = arrived(m)
    got_out[...] = got[WIN : WIN + 8]
    alpha0 = got0[0:1]
    alpha = got[WIN : WIN + 1]
    beta = got[WIN + 1 : WIN + 2]
    scale = alpha0 + alpha * beta
    before = facing(ax, ay, (d0, d1, d2, d3))
    first = facing(ax, ay, (e0, e1, e2, e3))
    second = facing(ax, ay, (f0, f1, f2, f3))
    for i in range(4):
        mine = l0[rows(i)] - scale * l1[rows(i)] - alpha * l2[rows(i)]
        other = before[i] - scale * first[i] - alpha * second[i]
        z = blended(wt, i, window_t, got, mine, other)
        z_out[rows(i)] = z
        zb[rows(i)] = split(z)
    z_out.send()
    apply_schur(schur, zb, s_out, (g0, g1, g2, g3))
    rz = jnp.zeros((1, R), F32)
    zz = jnp.zeros((1, R), F32)
    zq = jnp.zeros((1, R), F32)
    for i in range(4):
        z = z_out[rows(i)]
        s = s1[rows(i)] + beta * s0[rows(i)].astype(F32)
        r = load[rows(i)].astype(F32) - scale * q0[rows(i)] - alpha * q1[rows(i)]
        rz += total(wt[i] * r * z)
        zz += total(z * s_out[rows(i)])
        zq += total(z * s)
    inner = jnp.concatenate([rz, zz, zq, jnp.zeros((PAD - 3, R), F32)], axis=0)
    msg_out[...] = jnp.broadcast_to(inner[None], (NY, PAD, R))


def update_kernel(got0, got1, z0, z1, q0, q1, load, x_out, p_out, q_out, r_out):
    alpha0 = got0[0:1]
    alpha = got1[0:1]
    beta = got1[1:2]
    for i in range(4):
        p = z1[rows(i)] + beta * z0[rows(i)]
        q = q1[rows(i)] + beta * q0[rows(i)]
        p_out[rows(i)] = p
        q_out[rows(i)] = q
        x_out[rows(i)] = alpha0 * z0[rows(i)] + alpha * p
        r_out[rows(i)] = load[rows(i)].astype(F32) - alpha0 * q0[rows(i)] - alpha * q


def last_kernel(ax, ay, m, got, s, f0, f1, f2, f3, z, p, q, x, r, x_out, r_out):
    inner = jnp.sum(m[...], axis=0)
    rz1 = got[2:3]
    pq1 = got[3:4]
    rz = inner[0:1]
    beta = rz / rz1
    pq = inner[1:2] + 2.0 * beta * inner[2:3] + beta * beta * pq1
    alpha = rz / pq
    for i, face in enumerate(facing(ax, ay, (f0, f1, f2, f3))):
        product = s[rows(i)] + face + beta * q[rows(i)]
        direction = z[rows(i)] + beta * p[rows(i)]
        x_out[rows(i)] = (x[rows(i)] + alpha * direction).astype(BF16)
        r_out[rows(i)] = (r[rows(i)] - alpha * product).astype(BF16)


def send_column(out, column, other):
    for r in range(SL):
        out[:, :, 128 * r : 128 * (r + 1)] = jnp.broadcast_to(column[r : r + 1][None], (NX, 1, 128))
    out[:, :, 128 * SL :] = jnp.broadcast_to(other[None], (NX, 1, 128))


def column_kernel(m, out):
    where = lanes((SL, 128))
    column = jnp.zeros((SL, 128), F32)
    inner = jnp.zeros((SL, 128), F32)
    for b in range(NY):
        value = m[b]
        column += rolled(jnp.where(where < WIN, value, 0.0), 8 * (b - 1))
        inner += jnp.where((where >= WIN) & (where < WIN + 16), value, 0.0)
    other = jnp.zeros((1, 128), F32)
    for r in range(SL):
        other += rolled(inner[r : r + 1], 16 * r - WIN)
    send_column(out, column, other)


def first_column_kernel(m, out):
    where = lanes((SL, 128))
    column = jnp.zeros((SL, 128), F32)
    other = jnp.zeros((SL, 128), F32)
    for b in range(NY):
        value = m[b].astype(F32)
        value = value[0:SL] + value[SL : 2 * SL] + value[2 * SL : 3 * SL]
        column += rolled(jnp.where(where < WIN, value, 0.0), 8 * (b - 1))
        named = jnp.where((where >= 64) & (where < 66), value, 0.0)
        other += rolled(named, 8 * b - 64)
    send_column(out, column, other[0:1])


def unpacked(m, columns):
    for r in range(SL):
        columns[:, r : r + 1] = m[:, :, 128 * r : 128 * (r + 1)]


def vertex_sums(columns, group):
    place_of = lanes((SL, 128)) % 8 // 2
    result = jnp.zeros((SL, 128), F32)
    for k in range(4):
        value = jnp.zeros((SL, 128), F32)
        for j in range(4):
            value += rolled(columns[(4 * group + k - j + 1) % NX], 2 * (k - j))
        result += jnp.where(place_of == k, value, 0.0)
    return result


def reply(out, y, scalars):
    where = lanes((SL, 128))
    rest = jnp.zeros((SL, 128), F32)
    for j, value in enumerate(scalars):
        rest += jnp.where(where == WIN + j, value, 0.0)
    for b in range(NY):
        out[b] = jnp.where(where < WIN, rolled(y, -8 * (b - 1)), rest)


def solve(sums, table, out, scalars):
    y = dot(sums[...].astype(BF16), table[...])
    reply(out, y.astype(BF16).astype(F32), scalars)


def first_solve_kernel(ax, m, mine, other, sums, table, out, columns, picked, spread):
    unpacked(m, columns)
    for group in range(8):
        sums[:, 128 * group : 128 * (group + 1)] = vertex_sums(columns, group)
    own = jnp.zeros((1, 128), F32)
    for j in range(4):
        own += rolled(m[(ax[0] + j - 1 + NX) % NX, :, 128 * SL :], 2 * j)
    for i in range(4):
        number = lax.broadcasted_iota(jnp.int32, (FACE, 128), 0).astype(F32) + float(FACE * i)
        spread[rows(i), 0:128] = jnp.where(number == own, 1.0, 0.0).astype(BF16)
    for half, inverse in enumerate((mine, other)):
        value = jnp.zeros((NCG // 2, 128), F32)
        for k in range(8):
            block = inverse[:, 32 * k : 32 * (k + 1)].reshape(NCG // 2, 128)
            value += dot(block, spread[128 * k : 128 * (k + 1), 0:128])
        picked[NCG // 2 * half : NCG // 2 * (half + 1)] = value.astype(BF16)
    core = ax[0] % 2
    lane = lanes((128, 128))
    for group in range(8):
        named = jnp.zeros((1, 128), F32)
        for k in range(4):
            named += rolled(m[4 * group + k, :, 128 * SL :], 2 * k)
        named = jnp.transpose(jnp.broadcast_to(named, (128, 128))).astype(jnp.int32)
        far = jnp.where(((named >> 5) & 1) != core, NCG // 2, 0)
        named = ((named >> 6) << 5) + (named & 31) + far
        for part in range(8):
            spread[128 * group : 128 * (group + 1), 128 * part : 128 * (part + 1)] = jnp.where(
                named == lane + 128 * part, 1.0, 0.0
            ).astype(BF16)
    for i in range(4):
        table[rows(i)] = dot(spread[rows(i)], picked[...]).astype(BF16)
    solve(sums, table, out, ())


def inner_sums(m, count):
    inner = jnp.sum(m[:, :, 128 * SL :], axis=0)
    offset = lanes((SL, 128)) - 16 * lax.broadcasted_iota(jnp.int32, (SL, 128), 0)
    return [
        jnp.sum(jnp.where(offset == j, inner, 0.0), axis=1, keepdims=True) for j in range(count)
    ]


def second_solve_kernel(m, sums0, table, change, sums, kept, out, columns):
    rz, pq = inner_sums(m, 2)
    alpha = rz / pq
    unpacked(m, columns)
    for group in range(8):
        part = slice(128 * group, 128 * (group + 1))
        value = vertex_sums(columns, group)
        change[:, part] = value
        sums[:, part] = sums0[:, part] - alpha * value
    kept[...] = jnp.where(lanes((SL, 128)) == 0, rz, pq)
    solve(sums, table, out, (alpha,))


def third_solve_kernel(m, sums1, table, change0, kept, out, columns, sums):
    rz, zz, zq = inner_sums(m, 3)
    beta = rz / kept[:, 0:1]
    pq = zz + 2.0 * beta * zq + beta * beta * kept[:, 1:2]
    alpha = rz / pq
    unpacked(m, columns)
    for group in range(8):
        part = slice(128 * group, 128 * (group + 1))
        value = vertex_sums(columns, group) + beta * change0[:, part]
        sums[:, part] = sums1[:, part] - alpha * value
    solve(sums, table, out, (alpha, beta, rz, pq))


def last_column_kernel(m, out):
    out[...] = jnp.broadcast_to(jnp.sum(m[...], axis=0)[None], (NX, 8, R))


def across(axis, low, high):
    size = {"gx": NX, "gy": NY}[axis]
    up = [(i, (i + 1) % size) for i in range(size)]
    down = [(j, i) for i, j in up]
    return lax.ppermute(high, axis, up), lax.ppermute(low, axis, down)


def all_across(low_x, high_x, low_y, high_y):
    y = across("gy", low_y, high_y)
    return *across("gx", low_x, high_x), *y


def together(*values):
    return lax.optimization_barrier(values)


def swap(value, axis):
    return lax.all_to_all(value, axis, 0, 0, tiled=True)


def body(load_cases, schur_blocks, local_inverse, coarse_basis, corner_ids, coarse_inverse):
    load = load_cases[0, 0]
    schur = schur_blocks[0, 0]
    inverse = local_inverse[0, 0]
    basis = coarse_basis[0, 0]
    ids = corner_ids[0, 0]
    here = [lax.axis_index(axis).astype(jnp.int32).reshape(1) for axis in ("gx", "gy")]

    tall = (NI, R)
    msg = ((NY, SL, 128), F32)
    padded = ((NY, PAD, 128), F32)
    wide = ((NX, 1, LONG), F32)
    columns = pltpu.VMEM((NX, SL, 128), F32)
    block = 2 * NI * NI * R
    table = pltpu.VMEM((128, 128), F32)
    zb = pltpu.VMEM((NI, 2 * R), BF16)
    face = ((FACE, R), F32)

    l0, f0, f1, f2, f3, m = call(
        start_kernel,
        (*here, ids, load, basis, inverse, coarse_inverse),
        [(tall, F32)] + [((FACE + 16, R), F32)] * 4 + [((NY, FACE + 32, 128), BF16)],
        [table, pltpu.VMEM((WIN, NI), F32)],
        smem=3,
        flops=block,
    )
    faces0 = all_across(f0, f1, f2, f3)
    fx0, fx1, fy0, fy1 = faces0
    fy0, fy1, fx0, fx1, mine = together(fy0, fy1, fx0, fx1, swap(m, "gy"))
    faces0 = (fx0, fx1, fy0, fy1)
    other = lax.ppermute(mine, "gx", [(i, i ^ 1) for i in range(NX)])
    (m,) = call(first_column_kernel, (Part(mine, FACE, 32),), [wide], limit=SOME_BYTES)
    m = swap(m, "gx")
    window, window_t = call(
        window_kernel,
        (*here, basis, *faces0),
        [((2 * WIN, NI), BF16), ((NI, 2 * WIN), BF16)],
        [pltpu.VMEM((2 * WIN, NI), F32)],
        smem=2,
    )
    sums0, picked, m = call(
        first_solve_kernel,
        (here[0], Near(together(m, window)[0]), Near(mine), Near(other)),
        [((SL, NCG), F32), ((NCG, 128), BF16), msg],
        [columns, pltpu.VMEM((NCG, 128), BF16), pltpu.VMEM((NCG, NCG), BF16)],
        smem=1,
        flops=2 * block,
        limit=SOME_BYTES,
    )
    m = swap(m, "gy")
    z0, s0, g0, g1, g2, g3, m = call(
        first_kernel,
        (*here, m, window_t, l0, *faces0, schur, window, load),
        [(tall, F32), (tall, BF16)] + [((FACE, R), BF16)] * 4 + [padded],
        [table, pltpu.VMEM(tall, BF16)],
        smem=2,
        flops=block,
    )

    def stage(s, faces, m):
        fx0, fx1, fy0, fy1 = all_across(*faces)
        fy0, fy1, fx0, fx1, m = together(fy0, fy1, fx0, fx1, swap(m, "gy"))
        faces = (fx0, fx1, fy0, fy1)
        (m,) = call(column_kernel, (Part(m, 0, SL),), [wide], limit=SOME_BYTES)
        q, l, *faces = call(
            local_kernel,
            (*here, s, *faces, inverse),
            [(tall, F32), (tall, F32)] + [face] * 4,
            smem=2,
            flops=block,
        )
        fx0, fx1, fy0, fy1 = all_across(*faces)
        fy0, fy1, fx0, fx1, m = together(fy0, fy1, fx0, fx1, swap(m, "gx"))
        faces = (fx0, fx1, fy0, fy1)
        return m, q, l, faces

    m, q0, l1, faces1 = stage(s0, (g0, g1, g2, g3), m)
    change0, sums1, kept, m = call(
        second_solve_kernel,
        (Near(m), sums0, picked),
        [((SL, NCG), F32), ((SL, NCG), F32), ((SL, 128), F32), msg],
        [columns],
        limit=SOME_BYTES,
    )
    m = swap(m, "gy")
    z1, s1, g0, g1, g2, g3, m, got0 = call(
        second_kernel,
        (*here, m, window_t, l0, *faces0, l1, *faces1, schur, window, q0, s0, load),
        [(tall, F32), (tall, F32)] + [face] * 4 + [padded, ((8, R), F32)],
        [table, zb],
        smem=2,
        flops=block,
    )

    m, q1, l2, faces2 = stage(s1, (g0, g1, g2, g3), m)
    (m,) = call(
        third_solve_kernel,
        (Near(m), sums1, picked, change0, kept),
        [msg],
        [columns, pltpu.VMEM((SL, NCG), F32)],
        limit=SOME_BYTES,
    )
    m = swap(m, "gy")
    z2, s2, g0, g1, g2, g3, m, got1 = call(
        third_kernel,
        (
            *here, m, got0, window_t, l0, *faces0, l1, *faces1, l2, *faces2,
            schur, q0, q1, s0, s1, load,
        ),
        [(tall, F32), (tall, F32)] + [face] * 4 + [padded, ((8, R), F32)],
        [zb],
        smem=2,
        flops=block,
    )

    m, *faces, g2, g3, z0 = together(swap(m, "gy"), *across("gx", g0, g1), g2, g3, z0)
    (sums,) = call(last_column_kernel, (Part(m, 0, SL),), [((NX, 8, R), F32)], limit=SOME_BYTES)
    faces += across("gy", g2, g3)
    x2, p1, q1, r2 = call(
        update_kernel,
        (got0, got1, z0, z1, q0, q1, load),
        [(tall, F32)] * 4,
        flops=block,
    )
    m = swap(sums, "gx")
    x, r = call(
        last_kernel,
        (*here, m, got1, s2, *faces, z2, p1, q1, x2, r2),
        [(tall, BF16), (tall, BF16)],
        smem=2,
    )
    return x[None, None], r[None, None]


def solution(mesh):
    return jax.shard_map(
        body,
        mesh=mesh,
        in_specs=(
            P("gx", "gy", None, None),
            P("gx", "gy", None, None),
            P("gx", "gy", None, None),
            P("gx", "gy", None, None),
            P("gx", "gy", None),
            P("gy", None),
        ),
        out_specs=(P("gx", "gy", None, None), P("gx", "gy", None, None)),
        check_vma=False,
    )
```

```python
from typing import NamedTuple

import jax
import jax.numpy as jnp
from jax import lax
from jax.experimental import pallas as pl
from jax.experimental.pallas import tpu as pltpu
from jax.sharding import PartitionSpec as P

F32 = jnp.float32
BF16 = jnp.bfloat16
NI = 1024
FACE = 256
R = 128
NX = 32
NY = 16
SL = R // NY
NCG = 1024
VMEM_BYTES = 60 * 1024 * 1024
SOME_BYTES = 16 * 1024 * 1024
PAD = 16
LONG = SL * 128 + 128
WIN = 32

ANY = pl.BlockSpec(memory_space=pl.ANY)
VMEM = pl.BlockSpec(memory_space=pltpu.VMEM)
SMEM = pl.BlockSpec(memory_space=pltpu.SMEM)


class Taken:
    def __init__(self, source, buffer, semaphore):
        self.buffer = buffer
        self.copy = pltpu.make_async_copy(source, buffer, semaphore)
        self.copy.start()
        self.here = False

    def wait(self):
        if not self.here:
            self.copy.wait()
            self.here = True

    def __getitem__(self, index):
        self.wait()
        return self.buffer[index]

    def rows(self, first, size):
        self.wait()
        return self.buffer[pl.ds(pl.multiple_of(first, size), size)]


class Given:
    def __init__(self, target, buffer, semaphore):
        self.buffer = buffer
        self.copy = pltpu.make_async_copy(buffer, target, semaphore)
        self.sent = False

    def send(self):
        if not self.sent:
            self.copy.start()
            self.sent = True

    def __getitem__(self, index):
        return self.buffer[index]

    def __setitem__(self, index, value):
        self.buffer[index] = value


class Part(NamedTuple):
    array: jax.Array
    first: int
    size: int

    def shape(self):
        *blocks, _, width = self.array.shape
        return (*blocks, self.size, width)

    def of(self, ref):
        rows = pl.ds(self.first, self.size)
        return ref.at[rows] if self.array.ndim == 2 else ref.at[:, rows]


class Near(NamedTuple):
    array: jax.Array


class Small(NamedTuple):
    shape: tuple
    dtype: jnp.dtype


def call(kernel, args, outs, scratch=(), smem=0, flops=0, limit=VMEM_BYTES):
    inputs = args[smem:]
    count = len(inputs)
    parts = [a if isinstance(a, Part) else None for a in inputs]
    near = [isinstance(a, Near) for a in inputs] + [isinstance(t, Small) for t in outs]
    args = [a.array if isinstance(a, (Part, Near)) else a for a in args]
    size = sum(a.size * a.dtype.itemsize for a in args)
    shapes = [
        a.shape if part is None else part.shape() for a, part in zip(args[smem:], parts)
    ]
    whole = count + len(outs)

    def moved(*refs):
        scalars, refs = refs[:smem], refs[smem:]
        outside, buffers = refs[:whole], refs[whole : 2 * whole]
        semaphores, rest = refs[2 * whole], refs[2 * whole + 1 :]
        sources = [
            ref if part is None else part.of(ref) for ref, part in zip(outside, parts)
        ]
        moving = [i for i in range(whole) if not near[i]]
        values = list(outside)
        for i in moving:
            if i < count:
                values[i] = Taken(sources[i], buffers[i], semaphores.at[i])
            else:
                values[i] = Given(outside[i], buffers[i], semaphores.at[i])
        kernel(*scalars, *values, *rest)
        for i in moving:
            if i >= count:
                values[i].send()
        for i in moving:
            if i < count:
                values[i].wait()
            else:
                values[i].copy.wait()

    return pl.pallas_call(
        moved,
        out_shape=tuple(jax.ShapeDtypeStruct(*t) for t in outs),
        in_specs=[SMEM] * smem + [VMEM if n else ANY for n in near[:count]],
        out_specs=tuple(VMEM if n else ANY for n in near[count:]),
        scratch_shapes=[
            pltpu.VMEM((8, 128) if n else t, a.dtype)
            for n, t, a in zip(near, shapes, args[smem:])
        ]
        + [pltpu.VMEM((8, 128) if n else t[0], t[1]) for n, t in zip(near[count:], outs)]
        + [pltpu.SemaphoreType.DMA((whole,))]
        + list(scratch),
        compiler_params=pltpu.CompilerParams(vmem_limit_bytes=limit),
        cost_estimate=pl.CostEstimate(flops=flops, bytes_accessed=size, transcendentals=0),
    )(*args)


def rows(i):
    return slice(FACE * i, FACE * (i + 1))


def dot(a, b):
    return jnp.dot(a, b, preferred_element_type=F32)


def lanes(shape):
    return lax.broadcasted_iota(jnp.int32, shape, len(shape) - 1)


def rolled(value, shift):
    shift = shift % 128
    return value if shift == 0 else pltpu.roll(value, shift, value.ndim - 1)


def total(value):
    return jnp.sum(value, axis=0, keepdims=True)


def place(out, base, column, piece, dx0, dy0):
    width = piece.shape[1]
    for cx in range(2):
        for cy in range(2):
            row = base + (dy0 + cy) * 8 + (dx0 + cx) * 2
            slot = 4 * cx + 2 * cy
            out[row : row + 2, column : column + width] = piece[slot : slot + 2]


def shared(ax, ay):
    return ax[0] > 0, ax[0] < NX - 1, ay[0] > 0, ay[0] < NY - 1


def weights(ax, ay):
    return [jnp.where(face, 0.5, 1.0).astype(F32) for face in shared(ax, ay)]


def facing(ax, ay, faces):
    return [
        jnp.where(there, face[0:FACE].astype(F32), 0.0)
        for there, face in zip(shared(ax, ay), faces)
    ]


def thirds(value):
    high = value.astype(BF16).astype(F32)
    middle = (value - high).astype(BF16).astype(F32)
    return high, middle, value - high - middle


def start_kernel(
    ax, ay, ids, load, basis, inverse, coarse, l_out, f0, f1, f2, f3, msg_out, table, own
):
    wt = weights(ax, ay)
    piece = coarse.rows(32 * (ax[0] % 2), 32)
    for k in range(8):
        column = piece[:, 128 * k : 128 * (k + 1)]
        msg_out[:, 32 * k : 32 * (k + 1)] = jnp.broadcast_to(column[None], (NY, 32, 128))
    scaled = [(load[rows(i)].astype(F32) * wt[i]).astype(BF16) for i in range(4)]
    scaled = jnp.concatenate(scaled, axis=0)
    own[...] = jnp.zeros((WIN, NI), F32)
    place(own, 0, 0, basis[...].astype(F32), 1, 1)
    table[...] = jnp.zeros((128, 128), F32)
    table[0:WIN] = dot(own[...].astype(BF16), scaled)
    for c in range(2):
        table[64 + c : 65 + c] = jnp.full((1, 128), ids[c].astype(F32))
    terms = thirds(jnp.transpose(table[...]).reshape(NY, SL, 128))
    terms = jnp.concatenate([*terms, jnp.zeros((NY, SL, 128), F32)], axis=1)
    msg_out[:, FACE : FACE + 32] = terms.astype(BF16)
    msg_out.send()
    for i, face in enumerate((f0, f1, f2, f3)):
        local = wt[i] * dot(inverse[rows(i)], scaled)
        l_out[rows(i)] = local
        face[0:FACE] = local
        face[FACE : FACE + 8] = basis[:, FACE * i : FACE * i + 128].astype(F32)
        face[FACE + 8 : FACE + 16] = basis[:, FACE * i + 128 : FACE * (i + 1)].astype(F32)
        face.send()


def window_kernel(ax, ay, basis, f0, f1, f2, f3, b_out, bt_out, table):
    table[...] = jnp.zeros((2 * WIN, NI), F32)
    place(table, 0, 0, basis[...].astype(F32), 1, 1)
    there = shared(ax, ay)
    for i, (face, dx0, dy0) in enumerate(((f0, 0, 1), (f1, 2, 1), (f2, 1, 0), (f3, 1, 2))):
        for h in range(2):
            piece = jnp.where(there[i], face[FACE + 8 * h : FACE + 8 * h + 8], 0.0)
            place(table, WIN, FACE * i + 128 * h, piece, dx0, dy0)
    b_out[...] = table[...].astype(BF16)
    bt_out[...] = jnp.transpose(table[...]).astype(BF16)


def local_kernel(ax, ay, s, f0, f1, f2, f3, inverse, q_out, l_out, g0, g1, g2, g3):
    wt = weights(ax, ay)
    parts = []
    for i, face in enumerate(facing(ax, ay, (f0, f1, f2, f3))):
        q = s[rows(i)].astype(F32) + face
        q_out[rows(i)] = q
        parts.append((wt[i] * q).astype(BF16))
    q_out.send()
    scaled = jnp.concatenate(parts, axis=0)
    for i, face in enumerate((g0, g1, g2, g3)):
        local = wt[i] * dot(inverse[rows(i)], scaled)
        l_out[rows(i)] = local
        face[...] = local.astype(BF16)
        face.send()


def arrived(m):
    return jnp.transpose(m[...].reshape(R, 128))


def blended(wt, i, window_t, y, mine, other):
    y = y[0:WIN].astype(BF16)
    mine = mine + wt[i] * dot(window_t[rows(i), 0:WIN], y)
    other = other + wt[i] * dot(window_t[rows(i), WIN:], y)
    return mine.astype(BF16).astype(F32) + other.astype(BF16).astype(F32)


def split(value):
    high = value.astype(BF16)
    return jnp.concatenate([high, (value - high.astype(F32)).astype(BF16)], axis=1)


def joined(value):
    return value[:, 0:R] + value[:, R:]


def apply_schur(schur, zb, s_out, faces):
    for i in range(4):
        s = joined(dot(schur[rows(i)], zb[...]))
        s_out[rows(i)] = s
        if faces:
            faces[i][...] = s.astype(BF16)
            faces[i].send()
    s_out.send()


def window_terms(wt, window, s):
    terms = jnp.zeros((2 * WIN, 2 * R), F32)
    for i in range(4):
        terms += dot(window[:, rows(i)], split(s[rows(i)].astype(F32) * wt[i]))
    return joined(terms[0:WIN] + terms[WIN:])


def send_table(table, msg_out, terms, inner):
    table[...] = jnp.zeros((128, 128), F32)
    table[0:WIN] = terms
    for j, value in enumerate(inner):
        table[WIN + j : WIN + j + 1] = value
    msg_out[:, 0:SL] = jnp.transpose(table[...]).reshape(NY, SL, 128)
    msg_out[:, SL:] = jnp.zeros((NY, PAD - SL, 128), F32)


def first_kernel(
    ax, ay, m, window_t, l0, f0, f1, f2, f3, schur, window, load,
    z_out, s_out, g0, g1, g2, g3, msg_out, table, zb,
):
    wt = weights(ax, ay)
    y = arrived(m)
    for i, face in enumerate(facing(ax, ay, (f0, f1, f2, f3))):
        z = blended(wt, i, window_t, y, l0[rows(i)], face)
        z_out[rows(i)] = z
        zb[rows(i)] = z.astype(BF16)
    z_out.send()
    for i, face in enumerate((g0, g1, g2, g3)):
        s = dot(schur[rows(i)], zb[...]).astype(BF16)
        s_out[rows(i)] = s
        face[...] = s
        face.send()
    s_out.send()
    rz = jnp.zeros((1, R), F32)
    pq = jnp.zeros((1, R), F32)
    for i in range(4):
        z = z_out[rows(i)]
        rz += total(wt[i] * load[rows(i)].astype(F32) * z)
        pq += total(z * s_out[rows(i)].astype(F32))
    send_table(table, msg_out, window_terms(wt, window, s_out), (rz, pq))


def second_kernel(
    ax, ay, m, window_t, l0, e0, e1, e2, e3, l1, f0, f1, f2, f3, schur, window, q0, s0, load,
    z_out, s_out, g0, g1, g2, g3, msg_out, got_out, table, zb,
):
    wt = weights(ax, ay)
    got = arrived(m)
    got_out[...] = got[WIN : WIN + 8]
    alpha = got[WIN : WIN + 1]
    before = facing(ax, ay, (e0, e1, e2, e3))
    first = facing(ax, ay, (f0, f1, f2, f3))
    for i in range(4):
        mine = l0[rows(i)] - alpha * l1[rows(i)]
        z = blended(wt, i, window_t, got, mine, before[i] - alpha * first[i])
        z_out[rows(i)] = z
        zb[rows(i)] = split(z)
    z_out.send()
    apply_schur(schur, zb, s_out, (g0, g1, g2, g3))
    rz = jnp.zeros((1, R), F32)
    zz = jnp.zeros((1, R), F32)
    zq = jnp.zeros((1, R), F32)
    for i in range(4):
        z = z_out[rows(i)]
        r = load[rows(i)].astype(F32) - alpha * q0[rows(i)]
        rz += total(wt[i] * r * z)
        zz += total(z * s_out[rows(i)])
        zq += total(z * s0[rows(i)].astype(F32))
    send_table(table, msg_out, window_terms(wt, window, s_out), (rz, zz, zq))


def third_kernel(
    ax, ay, m, got0, window_t, l0, d0, d1, d2, d3, l1, e0, e1, e2, e3, l2, f0, f1, f2, f3,
    schur, q0, q1, s0, s1, load,
    z_out, s_out, g0, g1, g2, g3, msg_out, got_out, zb,
):
    wt = weights(ax, ay)
    got = arrived(m)
    got_out[...] = got[WIN : WIN + 8]
    alpha0 = got0[0:1]
    alpha = got[WIN : WIN + 1]
    beta = got[WIN + 1 : WIN + 2]
    scale = alpha0 + alpha * beta
    before = facing(ax, ay, (d0, d1, d2, d3))
    first = facing(ax, ay, (e0, e1, e2, e3))
    second = facing(ax, ay, (f0, f1, f2, f3))
    for i in range(4):
        mine = l0[rows(i)] - scale * l1[rows(i)] - alpha * l2[rows(i)]
        other = before[i] - scale * first[i] - alpha * second[i]
        z = blended(wt, i, window_t, got, mine, other)
        z_out[rows(i)] = z
        zb[rows(i)] = split(z)
    z_out.send()
    apply_schur(schur, zb, s_out, (g0, g1, g2, g3))
    rz = jnp.zeros((1, R), F32)
    zz = jnp.zeros((1, R), F32)
    zq = jnp.zeros((1, R), F32)
    for i in range(4):
        z = z_out[rows(i)]
        s = s1[rows(i)] + beta * s0[rows(i)].astype(F32)
        r = load[rows(i)].astype(F32) - scale * q0[rows(i)] - alpha * q1[rows(i)]
        rz += total(wt[i] * r * z)
        zz += total(z * s_out[rows(i)])
        zq += total(z * s)
    inner = jnp.concatenate([rz, zz, zq, jnp.zeros((PAD - 3, R), F32)], axis=0)
    msg_out[...] = jnp.broadcast_to(inner[None], (NY, PAD, R))


def update_kernel(got0, got1, z0, z1, q0, q1, load, x_out, p_out, q_out, r_out):
    alpha0 = got0[0:1]
    alpha = got1[0:1]
    beta = got1[1:2]
    for i in range(4):
        p = z1[rows(i)] + beta * z0[rows(i)]
        q = q1[rows(i)] + beta * q0[rows(i)]
        p_out[rows(i)] = p
        q_out[rows(i)] = q
        x_out[rows(i)] = alpha0 * z0[rows(i)] + alpha * p
        r_out[rows(i)] = load[rows(i)].astype(F32) - alpha0 * q0[rows(i)] - alpha * q


def last_kernel(ax, ay, m, got, s, f0, f1, f2, f3, z, p, q, x, r, x_out, r_out):
    inner = jnp.sum(m[...], axis=0)
    rz1 = got[2:3]
    pq1 = got[3:4]
    rz = inner[0:1]
    beta = rz / rz1
    pq = inner[1:2] + 2.0 * beta * inner[2:3] + beta * beta * pq1
    alpha = rz / pq
    for i, face in enumerate(facing(ax, ay, (f0, f1, f2, f3))):
        product = s[rows(i)] + face + beta * q[rows(i)]
        direction = z[rows(i)] + beta * p[rows(i)]
        x_out[rows(i)] = (x[rows(i)] + alpha * direction).astype(BF16)
        r_out[rows(i)] = (r[rows(i)] - alpha * product).astype(BF16)


def send_column(out, column, other):
    for r in range(SL):
        out[:, :, 128 * r : 128 * (r + 1)] = jnp.broadcast_to(column[r : r + 1][None], (NX, 1, 128))
    out[:, :, 128 * SL :] = jnp.broadcast_to(other[None], (NX, 1, 128))


def column_kernel(m, out):
    where = lanes((SL, 128))
    column = jnp.zeros((SL, 128), F32)
    inner = jnp.zeros((SL, 128), F32)
    for b in range(NY):
        value = m[b]
        column += rolled(jnp.where(where < WIN, value, 0.0), 8 * (b - 1))
        inner += jnp.where((where >= WIN) & (where < WIN + 16), value, 0.0)
    other = jnp.zeros((1, 128), F32)
    for r in range(SL):
        other += rolled(inner[r : r + 1], 16 * r - WIN)
    send_column(out, column, other)


def first_column_kernel(m, out):
    where = lanes((SL, 128))
    column = jnp.zeros((SL, 128), F32)
    other = jnp.zeros((SL, 128), F32)
    for b in range(NY):
        value = m[b].astype(F32)
        value = value[0:SL] + value[SL : 2 * SL] + value[2 * SL : 3 * SL]
        column += rolled(jnp.where(where < WIN, value, 0.0), 8 * (b - 1))
        named = jnp.where((where >= 64) & (where < 66), value, 0.0)
        other += rolled(named, 8 * b - 64)
    send_column(out, column, other[0:1])


def unpacked(m, columns):
    for r in range(SL):
        columns[:, r : r + 1] = m[:, :, 128 * r : 128 * (r + 1)]


def vertex_sums(columns, group):
    place_of = lanes((SL, 128)) % 8 // 2
    result = jnp.zeros((SL, 128), F32)
    for k in range(4):
        value = jnp.zeros((SL, 128), F32)
        for j in range(4):
            value += rolled(columns[(4 * group + k - j + 1) % NX], 2 * (k - j))
        result += jnp.where(place_of == k, value, 0.0)
    return result


def reply(out, y, scalars):
    where = lanes((SL, 128))
    rest = jnp.zeros((SL, 128), F32)
    for j, value in enumerate(scalars):
        rest += jnp.where(where == WIN + j, value, 0.0)
    for b in range(NY):
        out[b] = jnp.where(where < WIN, rolled(y, -8 * (b - 1)), rest)


def solve(sums, table, out, scalars):
    y = dot(sums[...].astype(BF16), table[...])
    reply(out, y.astype(BF16).astype(F32), scalars)


def first_solve_kernel(ax, m, mine, other, sums, table, out, columns, picked, spread):
    unpacked(m, columns)
    for group in range(8):
        sums[:, 128 * group : 128 * (group + 1)] = vertex_sums(columns, group)
    own = jnp.zeros((1, 128), F32)
    for j in range(4):
        own += rolled(m[(ax[0] + j - 1 + NX) % NX, :, 128 * SL :], 2 * j)
    for i in range(4):
        number = lax.broadcasted_iota(jnp.int32, (FACE, 128), 0).astype(F32) + float(FACE * i)
        spread[rows(i), 0:128] = jnp.where(number == own, 1.0, 0.0).astype(BF16)
    for half, inverse in enumerate((mine, other)):
        value = jnp.zeros((NCG // 2, 128), F32)
        for k in range(8):
            block = inverse[:, 32 * k : 32 * (k + 1)].reshape(NCG // 2, 128)
            value += dot(block, spread[128 * k : 128 * (k + 1), 0:128])
        picked[NCG // 2 * half : NCG // 2 * (half + 1)] = value.astype(BF16)
    core = ax[0] % 2
    lane = lanes((128, 128))
    for group in range(8):
        named = jnp.zeros((1, 128), F32)
        for k in range(4):
            named += rolled(m[4 * group + k, :, 128 * SL :], 2 * k)
        named = jnp.transpose(jnp.broadcast_to(named, (128, 128))).astype(jnp.int32)
        far = jnp.where(((named >> 5) & 1) != core, NCG // 2, 0)
        named = ((named >> 6) << 5) + (named & 31) + far
        for part in range(8):
            spread[128 * group : 128 * (group + 1), 128 * part : 128 * (part + 1)] = jnp.where(
                named == lane + 128 * part, 1.0, 0.0
            ).astype(BF16)
    for i in range(4):
        table[rows(i)] = dot(spread[rows(i)], picked[...]).astype(BF16)
    solve(sums, table, out, ())


def inner_sums(m, count):
    inner = jnp.sum(m[:, :, 128 * SL :], axis=0)
    offset = lanes((SL, 128)) - 16 * lax.broadcasted_iota(jnp.int32, (SL, 128), 0)
    return [
        jnp.sum(jnp.where(offset == j, inner, 0.0), axis=1, keepdims=True) for j in range(count)
    ]


def second_solve_kernel(m, sums0, table, change, sums, kept, out, columns):
    rz, pq = inner_sums(m, 2)
    alpha = rz / pq
    unpacked(m, columns)
    for group in range(8):
        part = slice(128 * group, 128 * (group + 1))
        value = vertex_sums(columns, group)
        change[:, part] = value
        sums[:, part] = sums0[:, part] - alpha * value
    kept[...] = jnp.where(lanes((SL, 128)) == 0, rz, pq)
    solve(sums, table, out, (alpha,))


def third_solve_kernel(m, sums1, table, change0, kept, out, columns, sums):
    rz, zz, zq = inner_sums(m, 3)
    beta = rz / kept[:, 0:1]
    pq = zz + 2.0 * beta * zq + beta * beta * kept[:, 1:2]
    alpha = rz / pq
    unpacked(m, columns)
    for group in range(8):
        part = slice(128 * group, 128 * (group + 1))
        value = vertex_sums(columns, group) + beta * change0[:, part]
        sums[:, part] = sums1[:, part] - alpha * value
    solve(sums, table, out, (alpha, beta, rz, pq))


def last_column_kernel(m, out):
    out[...] = jnp.broadcast_to(jnp.sum(m[...], axis=0)[None], (NX, 8, R))


def across(axis, low, high):
    size = {"gx": NX, "gy": NY}[axis]
    up = [(i, (i + 1) % size) for i in range(size)]
    down = [(j, i) for i, j in up]
    return lax.ppermute(high, axis, up), lax.ppermute(low, axis, down)


def all_across(low_x, high_x, low_y, high_y):
    y = across("gy", low_y, high_y)
    return *across("gx", low_x, high_x), *y


def together(*values):
    return lax.optimization_barrier(values)


def swap(value, axis):
    return lax.all_to_all(value, axis, 0, 0, tiled=True)


def body(load_cases, schur_blocks, local_inverse, coarse_basis, corner_ids, coarse_inverse):
    load = load_cases[0, 0]
    schur = schur_blocks[0, 0]
    inverse = local_inverse[0, 0]
    basis = coarse_basis[0, 0]
    ids = corner_ids[0, 0]
    here = [lax.axis_index(axis).astype(jnp.int32).reshape(1) for axis in ("gx", "gy")]

    tall = (NI, R)
    msg = ((NY, SL, 128), F32)
    padded = ((NY, PAD, 128), F32)
    wide = ((NX, 1, LONG), F32)
    columns = pltpu.VMEM((NX, SL, 128), F32)
    block = 2 * NI * NI * R
    table = pltpu.VMEM((128, 128), F32)
    zb = pltpu.VMEM((NI, 2 * R), BF16)
    face = ((FACE, R), BF16)

    l0, f0, f1, f2, f3, m = call(
        start_kernel,
        (*here, ids, load, basis, inverse, coarse_inverse),
        [(tall, F32)] + [((FACE + 16, R), F32)] * 4 + [((NY, FACE + 32, 128), BF16)],
        [table, pltpu.VMEM((WIN, NI), F32)],
        smem=3,
        flops=block,
    )
    faces0 = all_across(f0, f1, f2, f3)
    fx0, fx1, fy0, fy1 = faces0
    fy0, fy1, fx0, fx1, mine = together(fy0, fy1, fx0, fx1, swap(m, "gy"))
    faces0 = (fx0, fx1, fy0, fy1)
    other = lax.ppermute(mine, "gx", [(i, i ^ 1) for i in range(NX)])
    (m,) = call(first_column_kernel, (Part(mine, FACE, 32),), [wide], limit=SOME_BYTES)
    m = swap(m, "gx")
    window, window_t = call(
        window_kernel,
        (*here, basis, *faces0),
        [((2 * WIN, NI), BF16), ((NI, 2 * WIN), BF16)],
        [pltpu.VMEM((2 * WIN, NI), F32)],
        smem=2,
    )
    sums0, picked, m = call(
        first_solve_kernel,
        (here[0], Near(together(m, window)[0]), Near(mine), Near(other)),
        [((SL, NCG), F32), ((NCG, 128), BF16), msg],
        [columns, pltpu.VMEM((NCG, 128), BF16), pltpu.VMEM((NCG, NCG), BF16)],
        smem=1,
        flops=2 * block,
        limit=SOME_BYTES,
    )
    m = swap(m, "gy")
    z0, s0, g0, g1, g2, g3, m = call(
        first_kernel,
        (*here, m, window_t, l0, *faces0, schur, window, load),
        [(tall, F32), (tall, BF16)] + [((FACE, R), BF16)] * 4 + [padded],
        [table, pltpu.VMEM(tall, BF16)],
        smem=2,
        flops=block,
    )

    def stage(s, faces, m):
        fx0, fx1, fy0, fy1 = all_across(*faces)
        fy0, fy1, fx0, fx1, m = together(fy0, fy1, fx0, fx1, swap(m, "gy"))
        faces = (fx0, fx1, fy0, fy1)
        (m,) = call(column_kernel, (Part(m, 0, SL),), [wide], limit=SOME_BYTES)
        q, l, *faces = call(
            local_kernel,
            (*here, s, *faces, inverse),
            [(tall, F32), (tall, F32)] + [face] * 4,
            smem=2,
            flops=block,
        )
        fx0, fx1, fy0, fy1 = all_across(*faces)
        fy0, fy1, fx0, fx1, m = together(fy0, fy1, fx0, fx1, swap(m, "gx"))
        faces = (fx0, fx1, fy0, fy1)
        return m, q, l, faces

    m, q0, l1, faces1 = stage(s0, (g0, g1, g2, g3), m)
    change0, sums1, kept, m = call(
        second_solve_kernel,
        (Near(m), sums0, picked),
        [((SL, NCG), F32), ((SL, NCG), F32), ((SL, 128), F32), msg],
        [columns],
        limit=SOME_BYTES,
    )
    m = swap(m, "gy")
    z1, s1, g0, g1, g2, g3, m, got0 = call(
        second_kernel,
        (*here, m, window_t, l0, *faces0, l1, *faces1, schur, window, q0, s0, load),
        [(tall, F32), (tall, F32)] + [face] * 4 + [padded, ((8, R), F32)],
        [table, zb],
        smem=2,
        flops=block,
    )

    m, q1, l2, faces2 = stage(s1, (g0, g1, g2, g3), m)
    (m,) = call(
        third_solve_kernel,
        (Near(m), sums1, picked, change0, kept),
        [msg],
        [columns, pltpu.VMEM((SL, NCG), F32)],
        limit=SOME_BYTES,
    )
    m = swap(m, "gy")
    z2, s2, g0, g1, g2, g3, m, got1 = call(
        third_kernel,
        (
            *here, m, got0, window_t, l0, *faces0, l1, *faces1, l2, *faces2,
            schur, q0, q1, s0, s1, load,
        ),
        [(tall, F32), (tall, F32)] + [face] * 4 + [padded, ((8, R), F32)],
        [zb],
        smem=2,
        flops=block,
    )

    m, *faces, g2, g3, z0 = together(swap(m, "gy"), *across("gx", g0, g1), g2, g3, z0)
    (sums,) = call(last_column_kernel, (Part(m, 0, SL),), [((NX, 8, R), F32)], limit=SOME_BYTES)
    faces += across("gy", g2, g3)
    x2, p1, q1, r2 = call(
        update_kernel,
        (got0, got1, z0, z1, q0, q1, load),
        [(tall, F32)] * 4,
        flops=block,
    )
    m = swap(sums, "gx")
    x, r = call(
        last_kernel,
        (*here, m, got1, s2, *faces, z2, p1, q1, x2, r2),
        [(tall, BF16), (tall, BF16)],
        smem=2,
    )
    return x[None, None], r[None, None]


def solution(mesh):
    return jax.shard_map(
        body,
        mesh=mesh,
        in_specs=(
            P("gx", "gy", None, None),
            P("gx", "gy", None, None),
            P("gx", "gy", None, None),
            P("gx", "gy", None, None),
            P("gx", "gy", None),
            P("gy", None),
        ),
        out_specs=(P("gx", "gy", None, None), P("gx", "gy", None, None)),
        check_vma=False,
    )
```
